128 devices in a mesh: mpo: 4 (over x), bond: 32 (over y, z, core).
Axes of the slice: x: 4, y: 4, z: 4, core: 2. Of those that a mesh axis runs over, the one named last changes fastest.
Arguments:
- wavefunction: bfloat16 [4096, 4096], P('bond'), may hold values from -44 to 44
- subspace: bfloat16 [4, 4096, 4096], P(None, 'mpo', 'bond'), may hold values from -110 to 110
- left_band: bfloat16 [36, 4096, 320], P('mpo', 'bond'), may hold values from -3 to 3
- right_band: bfloat16 [36, 4096, 320], P('mpo', 'bond'), may hold values from -1 to 1
- left_sector: int32 [64], replicated, may hold values from 0 to 31, never falling along the last dimension, each value on 1 to 3 neighbouring positions
- right_sector: int32 [64], replicated, may hold values from 0 to 31, never falling along the last dimension, each value on 1 to 3 neighbouring positions
- term_sectors: int32 [36, 32], P('mpo'), may hold values 0 or 1
Outputs:
- applied: float32 [4096, 4096], P('mpo', 'bond')
- new_vector: float32 [4096, 4096], P('mpo', 'bond')
The draws below stay inside these ranges and needn't reach their ends.
Inputs may be any that keep to these rules, and one draw needn't show every extreme that they name: left_sector never falls; each sector covers 1 to 3 consecutive tiles, one exactly 3. right_sector never falls; each sector covers 1 to 3 consecutive tiles, one exactly 3.
All inputs are finite; a program needn't handle non-finite values. No bound on the sum of `term_sectors` on one device may be relied on, other than what follows from the above.
Results may differ from the reference program's by a relative error of at most 0.0023.
Values may be sent and summed in bfloat16 or wider, within the bound.
A program may use at most 128 MiB of HBM per device.

```python
import math
import jax
import jax.numpy as jnp
import numpy as np
from jax import lax

D_LEFT = 4096
D_RIGHT = 4096
TILE = 64
SEC_MOST = 3
K = 4
W = 36
BAND = 320
NTL = 64
NTR = 64
NSL = 32
NSR = 32


def shared_field(key):
    grid_key, row_key, column_key = jax.random.split(key, 3)
    rough = jnp.clip(jax.random.normal(grid_key, (D_LEFT, D_RIGHT), jnp.float32), -4.0, 4.0)
    field = rough
    rise = math.log(3.0)
    row_scale = jnp.exp(rise * jnp.arange(D_LEFT, dtype=jnp.float32) / D_LEFT + jax.random.uniform(row_key, (D_LEFT,), jnp.float32, 0.0, math.log(3.3))) / 3.0
    column_scale = jnp.exp(rise * jnp.arange(D_RIGHT, dtype=jnp.float32) / D_RIGHT + jax.random.uniform(column_key, (D_RIGHT,), jnp.float32, 0.0, math.log(3.3))) / 3.0
    return (field, row_scale[:, None] * column_scale[None, :])


def band_values(key, row_count, scale, diagonal_scale):
    noise_key, diagonal_key = jax.random.split(key, 2)
    values = jnp.clip(jax.random.normal(noise_key, (W, row_count, BAND), jnp.float32), -4.0, 4.0) * scale
    column = jnp.arange(BAND)[None, None, :]
    row_index = jnp.arange(row_count)[None, :, None]
    on_diagonal = column == (SEC_MOST - 1) * TILE + row_index % TILE
    diagonal = jnp.exp(jax.random.uniform(diagonal_key, (W, row_count, 1), jnp.float32, math.log(0.5), math.log(2.0))) * diagonal_scale
    return jnp.where(on_diagonal, values + diagonal, values)


def draw_wavefunction(key, part):
    field, scale = shared_field(key)
    return (scale * field).astype(jnp.bfloat16)


def draw_subspace(key, part):
    field, scale = shared_field(key)
    key = jax.random.fold_in(key, 2)
    weight_key, noise_key = jax.random.split(key, 2)
    factor = jax.random.uniform(weight_key, (K,), jnp.float32, 0.5, 1.5)
    rough = jnp.clip(jax.random.normal(noise_key, (K, D_LEFT, D_RIGHT), jnp.float32), -4.0, 4.0)
    noise = rough
    return (scale[None] * (factor[:, None, None] * field[None] + noise)).astype(jnp.bfloat16)


def draw_left_band(key, part):
    key = jax.random.fold_in(key, 3)
    return band_values(key, D_LEFT, (SEC_MOST * TILE) ** (-0.5), 1.0).astype(jnp.bfloat16)


def draw_right_band(key, part):
    key = jax.random.fold_in(key, 4)
    return band_values(key, D_RIGHT, (SEC_MOST * TILE * W) ** (-0.5), 1.0 / W).astype(jnp.bfloat16)


def set_ends(result, stream_key, smallest, largest):
    index_at = [jax.random.randint(jax.random.fold_in(stream_key, axis), (), 0, length) for axis, length in enumerate(result.shape)]
    main_axis = result.shape.index(max(result.shape))
    beside = index_at[:main_axis] + [(index_at[main_axis] + 1) % result.shape[main_axis]] + index_at[main_axis + 1:]
    return result.at[tuple(index_at)].set(smallest).at[tuple(beside)].set(largest)


def length_profile(count, total, limit, slope):
    weights = [(1 << 20) // math.isqrt(grade ** slope) + 1 for grade in range(2, count + 1)]
    surplus, given = total - limit - (count - 1), [1] * (count - 1)
    while surplus > 0:
        movable = [i for i in range(count - 1) if given[i] < limit]
        mass, budget = sum([weights[i] for i in movable]), surplus
        for i in movable:
            more = min(limit - given[i], max(1, budget * weights[i] // mass), surplus)
            given[i] = given[i] + more
            surplus = surplus - more
    return np.array([limit] + given)


def ragged_sizes(own_key, number_of, total, limit, skew):
    if number_of == 2:
        one = jax.random.randint(own_key, (), max(1, total - limit), min(limit, total - 1) + 1)
        return jnp.stack([one, total - one])
    lengths = jnp.asarray(length_profile(number_of, total, limit, skew), jnp.int32)
    couples = (number_of - 1) // 2
    source_of, sink = lengths[1:1 + 2 * couples:2], lengths[2:2 + 2 * couples:2]
    room = jnp.minimum(source_of - 1, limit - sink)
    moved = jax.random.randint(jax.random.fold_in(own_key, 1), (couples,), 0, 1 << 20) % (room + 1)
    lengths = lengths.at[1:1 + 2 * couples:2].set(source_of - moved).at[2:2 + 2 * couples:2].set(sink + moved)
    return lengths[jax.random.permutation(jax.random.fold_in(own_key, 2), number_of)]


def setup_inputs(seed: int = 0) -> dict:
    key_of = jax.random.split(jax.random.key(seed), 8)
    return {
        "wavefunction": draw_wavefunction(jax.random.fold_in(key_of[7], 71), 0),
        "subspace": draw_subspace(jax.random.fold_in(key_of[7], 71), 0),
        "left_band": draw_left_band(jax.random.fold_in(key_of[7], 71), 0),
        "right_band": draw_right_band(jax.random.fold_in(key_of[7], 71), 0),
        "left_sector": jnp.searchsorted(jnp.cumsum(ragged_sizes(key_of[4], NSL, NTL, SEC_MOST, 1)), jnp.arange(NTL), side="right").astype(jnp.int32),
        "right_sector": jnp.searchsorted(jnp.cumsum(ragged_sizes(key_of[5], NSR, NTR, SEC_MOST, 1)), jnp.arange(NTR), side="right").astype(jnp.int32),
        "term_sectors": set_ends((jax.random.randint(key_of[6], (W, NSL), 0, 4) < 3).astype(jnp.int32), jax.random.fold_in(key_of[6], 1), 0, 1),
    }


epsilon = 1e-06

def neighbour_sector(sector, offset):
    margin = SEC_MOST - 1
    filler = -jnp.ones((margin,), jnp.int32)
    padded = jnp.concatenate([filler, sector.astype(jnp.int32), filler])
    return lax.slice_in_dim(padded, offset, offset + sector.shape[0])

def left_apply(band_term, active_term, wavefunction, left_sector):
    margin = SEC_MOST - 1
    tile_count = D_LEFT // TILE
    source = wavefunction.astype(jnp.float32).reshape(tile_count, TILE, D_RIGHT)
    zero_tiles = jnp.zeros((margin, TILE, D_RIGHT), jnp.float32)
    source = jnp.concatenate([zero_tiles, source, zero_tiles])
    switched = active_term[left_sector] == 1
    running = jnp.zeros((tile_count, TILE, D_RIGHT), jnp.float32)
    for offset in range(2 * margin + 1):
        linked = (neighbour_sector(left_sector, offset) == left_sector) & switched
        blocks = band_term[:, offset * TILE:(offset + 1) * TILE].astype(jnp.float32)
        blocks = blocks.reshape(tile_count, TILE, TILE) * linked.astype(jnp.float32)[:, None, None]
        running = running + jnp.einsum('tij,tjc->tic', blocks, source[offset:offset + tile_count])
    return running.reshape(D_LEFT, D_RIGHT).astype(jnp.bfloat16)

def right_apply(band_term, middle, right_sector):
    margin = SEC_MOST - 1
    tile_count = D_RIGHT // TILE
    source = middle.astype(jnp.float32).reshape(D_LEFT, tile_count, TILE)
    spread = jnp.zeros((D_LEFT, tile_count + 2 * margin, TILE), jnp.float32)
    for offset in range(2 * margin + 1):
        linked = neighbour_sector(right_sector, offset) == right_sector
        blocks = band_term[:, offset * TILE:(offset + 1) * TILE].astype(jnp.float32)
        blocks = blocks.reshape(tile_count, TILE, TILE) * linked.astype(jnp.float32)[:, None, None]
        spread = spread.at[:, offset:offset + tile_count].add(jnp.einsum('rjc,jck->rjk', source, blocks))
    return spread[:, margin:margin + tile_count].reshape(D_LEFT, D_RIGHT)

def reference(wavefunction, subspace, left_band, right_band, left_sector, right_sector, term_sectors):

    def one_term(carried, members):
        band_left, band_right, active_term = members
        middle = left_apply(band_left, active_term, wavefunction, left_sector)
        return (carried + right_apply(band_right, middle, right_sector), None)
    initial = jnp.zeros((D_LEFT, D_RIGHT), jnp.float32)
    applied = lax.scan(one_term, initial, (left_band, right_band, term_sectors))[0]
    entries = D_LEFT * D_RIGHT
    highest = lax.Precision.HIGHEST
    vectors = subspace.astype(jnp.float32)
    correlation = jnp.einsum('kxy,xy->k', vectors, applied, precision=highest) / entries
    squares = jnp.einsum('kxy,kxy->k', vectors, vectors, precision=highest) / entries
    coefficient = correlation / (squares + epsilon)
    residual = applied - jnp.einsum('k,kxy->xy', coefficient, vectors, precision=highest)
    new_vector = residual * lax.rsqrt(jnp.mean(residual * residual) + epsilon)
    return (applied, new_vector)
```

```python
import jax
import jax.numpy as jnp
from jax import lax
from jax.experimental import pallas as pl
from jax.experimental.pallas import tpu as pltpu
from jax.sharding import PartitionSpec as P

D_LEFT = 4096
D_RIGHT = 4096
TILE = 64
SEC_MOST = 3
MARGIN = SEC_MOST - 1
SPANS = 2 * MARGIN + 1
PACKED = SEC_MOST * TILE
NT = D_RIGHT // TILE
CHUNKS = 3
MESH = pl.DeviceIdType.MESH

epsilon = 1e-06


def sector_starts(sector):
    same = sector[:, None] == sector[None, :]
    return jnp.argmax(same, axis=1).astype(jnp.int32)


def pack_kernel(place_ref, band_ref, mask_ref, out_ref):
    groups = band_ref.shape[0]
    for w in range(groups):
        halves = []
        for h in range(2):
            rows = band_ref[w, h * TILE : (h + 1) * TILE, :]
            p = place_ref[h]
            picked = jnp.where(
                p == 0,
                rows[:, 2 * TILE : 2 * TILE + PACKED],
                jnp.where(p == 1, rows[:, TILE : TILE + PACKED], rows[:, :PACKED]),
            )
            halves.append(picked * mask_ref[h : h + 1, :PACKED])
        out_ref[w] = jnp.concatenate(halves, axis=1)


def left_kernel(band_ref, mask_ref, prev_ref, own_ref, next_ref, out_ref, kept_ref):
    groups = band_ref.shape[0]

    @pl.when(pl.program_id(0) == 0)
    def _():
        for w in range(groups):
            for h in range(2):
                kept_ref[h, w * TILE : (w + 1) * TILE, :] = (
                    band_ref[w, h * TILE : (h + 1) * TILE, :] * mask_ref[w, h : h + 1, :]
                )

    rows = jnp.concatenate([prev_ref[...], own_ref[...], next_ref[...]], axis=0)
    for h in range(2):
        made = jnp.dot(
            kept_ref[h],
            rows[h * TILE : h * TILE + SPANS * TILE],
            preferred_element_type=jnp.float32,
        ).astype(jnp.bfloat16)
        for w in range(groups):
            out_ref[w, h * TILE : (h + 1) * TILE, :] = made[w * TILE : (w + 1) * TILE]


def right_kernel(blocks_each, first, start_ref, mid_ref, band_ref, *rest):
    if first:
        out_ref, total = rest
    else:
        part_ref, out_ref, total = rest
    step = pl.program_id(0)

    @pl.when(step == 0)
    def _():
        total[...] = jnp.zeros_like(total) if first else part_ref[...]

    terms = mid_ref.shape[0]
    lane = lax.broadcasted_iota(jnp.int32, (128, 256), 1)
    for b in range(blocks_each):
        for h in range(2):
            left = jnp.concatenate(
                [
                    mid_ref[w, :, b * 128 + h * TILE : b * 128 + (h + 1) * TILE]
                    for w in range(terms)
                ],
                axis=1,
            )
            right = band_ref[b, :, :, h * 128 : h * 128 + 256].reshape(terms * TILE, 256)
            made = jnp.dot(left, right, preferred_element_type=jnp.float32)
            start = start_ref[(step * blocks_each + b) * 2 + h]
            odd = lax.rem(start, 2)
            if h == 0:
                made = jnp.where(lane < PACKED, made, 0.0)
            else:
                made = jnp.where(lane >= TILE, made, 0.0)
            moved = pltpu.roll(made, TILE if h == 0 else 256 - TILE, 1)
            made = jnp.where(odd == h, made, moved)
            at = pl.ds(pl.multiple_of((start // 2) * 128, 128), 256)
            total[:, at] += made

    @pl.when(step == pl.num_programs(0) - 1)
    def _():
        out_ref[...] = total[...]


def finish_kernel(
    part_ref, sub_ref, applied_ref, vector_ref,
    out_a, in_a, out_b, app, mine, first_in, second_out, second_in,
    send_a, recv_a, send_b, recv_b, send_c, recv_c, send_d, recv_d,
):
    x = lax.axis_index("mpo")
    bond = lax.axis_index("bond")
    y = bond // 8
    q = lax.rem(bond, 8)

    barrier = pltpu.get_barrier_semaphore()
    for d in range(1, 8):
        pl.semaphore_signal(
            barrier, inc=1, device_id=(x, y * 8 + lax.rem(q + d, 8)), device_id_type=MESH
        )
    for d in range(1, 16):
        other = lax.rem(x * 4 + y + d, 16)
        pl.semaphore_signal(
            barrier, inc=1, device_id=(other // 4, lax.rem(other, 4) * 8 + q), device_id_type=MESH
        )

    @pl.when(x != y)
    def _():
        for k in range(8):
            pl.semaphore_signal(barrier, inc=1, device_id=(y, x * 8 + k), device_id_type=MESH)
        pl.semaphore_wait(barrier, 30)

    @pl.when(x == y)
    def _():
        pl.semaphore_wait(barrier, 22)

    copies_a = []
    for d in range(1, 4):
        j = lax.rem(x + d, 4)
        columns = pl.ds(pl.multiple_of(j * 1024, 1024), 1024)
        out_a[d - 1] = part_ref[:, columns].astype(jnp.bfloat16)
        copy = pltpu.make_async_remote_copy(
            src_ref=out_a.at[d - 1], dst_ref=in_a.at[d - 1],
            send_sem=send_a.at[d - 1], recv_sem=recv_a.at[d - 1],
            device_id=(j, bond), device_id_type=MESH,
        )
        copy.start()
        copies_a.append(copy)

    mine[...] = jnp.zeros_like(mine)
    row = 5
    for k in range(4):
        for m in range(k, 4):
            def gram(i, held, k=k, m=m):
                at = pl.ds(pl.multiple_of(i * 64, 64), 64)
                return held + jnp.sum(
                    (sub_ref[k, at, :].astype(jnp.float32) * sub_ref[m, at, :].astype(jnp.float32)).reshape(8, 8, 128),
                    axis=0,
                )
            held = lax.fori_loop(0, 16, gram, jnp.zeros((8, 128), jnp.float32))
            mine[row : row + 1, :] = jnp.sum(held, axis=0, keepdims=True)
            row += 1

    for copy in copies_a:
        copy.wait()

    own = pl.multiple_of(x * 1024, 1024)
    for k in range(8):
        at = pl.ds(pl.multiple_of(own + k * 128, 128), 128)
        out_b[k] = (
            part_ref[:, at]
            + in_a[0, :, k * 128 : (k + 1) * 128].astype(jnp.float32)
            + in_a[1, :, k * 128 : (k + 1) * 128].astype(jnp.float32)
            + in_a[2, :, k * 128 : (k + 1) * 128].astype(jnp.float32)
        )
        here = (x == y) & (q == k)

        @pl.when(jnp.logical_not(here))
        def _(k=k):
            pltpu.make_async_remote_copy(
                src_ref=out_b.at[k], dst_ref=app.at[q],
                send_sem=send_b.at[k], recv_sem=recv_b.at[q],
                device_id=(y, x * 8 + k), device_id_type=MESH,
            ).start()

        @pl.when(here)
        def _(k=k):
            app[k] = out_b[k]

    for k in range(8):
        here = (x == y) & (q == k)

        @pl.when(jnp.logical_not(here))
        def _(k=k):
            pltpu.make_async_remote_copy(
                src_ref=out_b.at[k], dst_ref=app.at[k],
                send_sem=send_b.at[k], recv_sem=recv_b.at[k],
                device_id=(y, x * 8 + k), device_id_type=MESH,
            ).wait()

    def sums(i, held):
        block = app[i]
        rows = pl.ds(pl.multiple_of(i * 128, 128), 128)
        new = [held[0] + jnp.sum((block * block).reshape(16, 8, 128), axis=0)]
        for k in range(4):
            product = sub_ref[k, rows, :].astype(jnp.float32) * block
            new.append(held[k + 1] + jnp.sum(product.reshape(16, 8, 128), axis=0))
        return tuple(new)

    held = lax.fori_loop(0, 8, sums, tuple(jnp.zeros((8, 128), jnp.float32) for _ in range(5)))
    for k in range(5):
        mine[k : k + 1, :] = jnp.sum(held[k], axis=0, keepdims=True)

    copies = []
    for d in range(1, 8):
        copy = pltpu.make_async_remote_copy(
            src_ref=mine, dst_ref=first_in.at[d - 1],
            send_sem=send_c.at[d - 1], recv_sem=recv_c.at[d - 1],
            device_id=(x, y * 8 + lax.rem(q + d, 8)), device_id_type=MESH,
        )
        copy.start()
        copies.append(copy)
    for copy in copies:
        copy.wait()
    added = mine[...]
    for d in range(7):
        added = added + first_in[d]
    second_out[...] = added
    copies = []
    for d in range(1, 16):
        other = lax.rem(x * 4 + y + d, 16)
        copy = pltpu.make_async_remote_copy(
            src_ref=second_out, dst_ref=second_in.at[d - 1],
            send_sem=send_d.at[d - 1], recv_sem=recv_d.at[d - 1],
            device_id=(other // 4, lax.rem(other, 4) * 8 + q), device_id_type=MESH,
        )
        copy.start()
        copies.append(copy)
    for copy in copies:
        copy.wait()
    for d in range(15):
        added = added + second_in[d]
    sums_all = jnp.sum(added, axis=1, keepdims=True)

    entries = float(D_LEFT * D_RIGHT)

    def one(i):
        return sums_all[i : i + 1, :] * (1.0 / entries)

    gram_at = {}
    row = 5
    for k in range(4):
        for m in range(k, 4):
            gram_at[k, m] = row
            row += 1
    coefficient = [one(1 + k) / (one(gram_at[k, k]) + epsilon) for k in range(4)]
    energy = one(0)
    for k in range(4):
        energy = energy - 2.0 * coefficient[k] * one(1 + k)
        for m in range(k, 4):
            twice = 1.0 if m == k else 2.0
            energy = energy + twice * coefficient[k] * coefficient[m] * one(gram_at[k, m])
    scale = lax.rsqrt(jnp.maximum(energy, 0.0) + epsilon)

    def write(i, carry):
        rows = pl.ds(pl.multiple_of(i * 128, 128), 128)
        block = app[i]
        residual = block
        for k in range(4):
            residual = residual - coefficient[k] * sub_ref[k, rows, :].astype(jnp.float32)
        applied_ref[rows, :] = block
        vector_ref[rows, :] = residual * scale
        return carry

    lax.fori_loop(0, 8, write, 0)


def per_device(
    wavefunction, subspace, left_band, right_band, left_sector, right_sector, term_sectors
):
    groups = left_band.shape[0]
    position = lax.axis_index("bond")
    count = lax.axis_size("bond")
    ends = count - 1

    before = lax.ppermute(wavefunction, "bond", [(i, i + 1) for i in range(ends)])
    after = lax.ppermute(wavefunction, "bond", [(i + 1, i) for i in range(ends)])

    filler = -jnp.ones((SPANS,), jnp.int32)
    right_start = sector_starts(right_sector)
    own_tiles = position * 2 + jnp.arange(2, dtype=jnp.int32)
    own_start = right_start[own_tiles]
    place = own_tiles - own_start
    right_padded = jnp.concatenate([right_sector, filler])
    in_sector = jnp.stack(
        [right_padded[own_start + m] == right_sector[own_tiles] for m in range(SEC_MOST)], axis=1
    )
    pack_mask = jnp.repeat(in_sector.astype(jnp.bfloat16), TILE, axis=1)
    packed = pl.pallas_call(
        pack_kernel,
        out_shape=jax.ShapeDtypeStruct((groups, TILE, 2 * PACKED), jnp.bfloat16),
        in_specs=[
            pl.BlockSpec(memory_space=pltpu.SMEM),
            pl.BlockSpec(memory_space=pltpu.VMEM),
            pl.BlockSpec(memory_space=pltpu.VMEM),
        ],
        out_specs=pl.BlockSpec(memory_space=pltpu.VMEM),
        compiler_params=pltpu.CompilerParams(vmem_limit_bytes=32 * 1024 * 1024),
        name="pack_right",
    )(place, right_band, pack_mask)

    each = groups // CHUNKS
    gathered = [
        lax.all_gather(packed[i * each : (i + 1) * each], "bond", axis=0, tiled=False)
        for i in range(CHUNKS)
    ]

    left_padded = jnp.concatenate([filler, left_sector, filler])
    own_left = left_sector[own_tiles]
    linked = jnp.stack(
        [left_padded[SPANS + own_tiles + o - MARGIN] == own_left for o in range(SPANS)], axis=1
    )
    active = term_sectors[:, own_left] == 1
    left_mask = jnp.repeat(
        (linked[None] & active[:, :, None]).astype(jnp.bfloat16), TILE, axis=2
    )
    width = 512
    middle = pl.pallas_call(
        left_kernel,
        grid=(D_RIGHT // width,),
        out_shape=jax.ShapeDtypeStruct((groups, 128, D_RIGHT), jnp.bfloat16),
        in_specs=[
            pl.BlockSpec((groups, 128, SPANS * TILE), lambda i: (0, 0, 0)),
            pl.BlockSpec((groups, 2, SPANS * TILE), lambda i: (0, 0, 0)),
            pl.BlockSpec((128, width), lambda i: (0, i)),
            pl.BlockSpec((128, width), lambda i: (0, i)),
            pl.BlockSpec((128, width), lambda i: (0, i)),
        ],
        out_specs=pl.BlockSpec((groups, 128, width), lambda i: (0, 0, i)),
        scratch_shapes=[pltpu.VMEM((2, groups * TILE, SPANS * TILE), jnp.bfloat16)],
        compiler_params=pltpu.CompilerParams(vmem_limit_bytes=48 * 1024 * 1024),
        cost_estimate=pl.CostEstimate(
            flops=2 * groups * 128 * 320 * 4096, bytes_accessed=14 << 20, transcendentals=0
        ),
        name="left_apply",
    )(left_band, left_mask, before, wavefunction, after)

    blocks_each = 4
    held = D_RIGHT + 128
    part = None
    for i in range(CHUNKS):
        operands = [right_start, middle, gathered[i]]
        in_specs = [
            pl.BlockSpec(memory_space=pltpu.SMEM),
            pl.BlockSpec((each, 128, blocks_each * 128), lambda s, i=i: (i, 0, s)),
            pl.BlockSpec((blocks_each, each, TILE, 2 * PACKED), lambda s: (s, 0, 0, 0)),
        ]
        if part is not None:
            operands.append(part)
            in_specs.append(pl.BlockSpec((128, held), lambda s: (0, 0)))
        part = pl.pallas_call(
            lambda *refs, first=part is None: right_kernel(blocks_each, first, *refs),
            grid=(32 // blocks_each,),
            out_shape=jax.ShapeDtypeStruct((128, held), jnp.float32),
            in_specs=in_specs,
            out_specs=pl.BlockSpec((128, held), lambda s: (0, 0)),
            scratch_shapes=[pltpu.VMEM((128, held), jnp.float32)],
            compiler_params=pltpu.CompilerParams(vmem_limit_bytes=48 * 1024 * 1024),
            cost_estimate=pl.CostEstimate(
                flops=2 * 64 * 128 * 192 * 256, bytes_accessed=12 << 20, transcendentals=0
            ),
            name="right_apply",
        )(*operands)

    shape = jax.ShapeDtypeStruct((1024, 128), jnp.float32)
    dma = pltpu.SemaphoreType.DMA
    return pl.pallas_call(
        finish_kernel,
        out_shape=(shape, shape),
        in_specs=[pl.BlockSpec(memory_space=pltpu.VMEM)] * 2,
        out_specs=(pl.BlockSpec(memory_space=pltpu.VMEM),) * 2,
        scratch_shapes=[
            pltpu.VMEM((3, 128, 1024), jnp.bfloat16),
            pltpu.VMEM((3, 128, 1024), jnp.bfloat16),
            pltpu.VMEM((8, 128, 128), jnp.float32),
            pltpu.VMEM((8, 128, 128), jnp.float32),
            pltpu.VMEM((16, 128), jnp.float32),
            pltpu.VMEM((7, 16, 128), jnp.float32),
            pltpu.VMEM((16, 128), jnp.float32),
            pltpu.VMEM((15, 16, 128), jnp.float32),
            dma((3,)), dma((3,)), dma((8,)), dma((8,)),
            dma((7,)), dma((7,)), dma((15,)), dma((15,)),
        ],
        compiler_params=pltpu.CompilerParams(
            collective_id=0, has_side_effects=True, vmem_limit_bytes=32 * 1024 * 1024
        ),
        name="finish",
    )(part, subspace)


def solution(mesh):
    return jax.shard_map(
        per_device,
        mesh=mesh,
        in_specs=(
            P("bond", None),
            P(None, "mpo", "bond"),
            P("mpo", "bond", None),
            P("mpo", "bond", None),
            P(),
            P(),
            P("mpo", None),
        ),
        out_specs=(P("mpo", "bond"), P("mpo", "bond")),
        check_vma=False,
    )
```

```python
import functools

import jax
import jax.numpy as jnp
from jax import lax
from jax.experimental import pallas as pl
from jax.experimental.pallas import tpu as pltpu
from jax.sharding import PartitionSpec as P

D_LEFT = 4096
D_RIGHT = 4096
TILE = 64
SEC_MOST = 3
PACKED = SEC_MOST * TILE
NT = 64
TERMS = 9
DEEP = TERMS * TILE
MESH = pl.DeviceIdType.MESH

epsilon = 1e-06


def as_int(flag):
    return flag.astype(jnp.int32)


def place_in_sector(sector, tile):
    here = sector[tile]
    one = as_int((tile >= 1) & (sector[jnp.maximum(tile - 1, 0)] == here))
    two = as_int((tile >= 2) & (sector[jnp.maximum(tile - 2, 0)] == here))
    return one + two


def sector_size(sector, tile):
    here = sector[tile]
    one = as_int((tile <= NT - 2) & (sector[jnp.minimum(tile + 1, NT - 1)] == here))
    two = as_int((tile <= NT - 3) & (sector[jnp.minimum(tile + 2, NT - 1)] == here))
    return 1 + place_in_sector(sector, tile) + one + two


def pack(band, packed, sector, first_tile, active):
    lane = lax.broadcasted_iota(jnp.int32, (TILE, PACKED), 1)
    info = []
    for h in range(2):
        tile = first_tile + h
        info.append((place_in_sector(sector, tile), sector_size(sector, tile), sector[tile]))
    chosen = []
    if active is not None:
        number = lax.broadcasted_iota(jnp.int32, active.shape, 1)
        for h in range(2):
            same = 1 - jnp.clip(jnp.abs(number - info[h][2]), 0, 1)
            chosen.append(jnp.sum(active[...] * same, axis=1, keepdims=True))
    for w in range(TERMS):
        halves = []
        for h in range(2):
            p, size, here = info[h]
            rows = band[w, h * TILE : (h + 1) * TILE, :]
            limit = size * TILE
            if active is not None:
                limit = limit * chosen[h][w : w + 1]
            picked = 0.0
            for at in range(SEC_MOST):
                kept = jnp.clip(limit * as_int(p == at) - lane, 0, 1).astype(jnp.bfloat16)
                first = (SEC_MOST - 1 - at) * TILE
                picked = picked + rows[:, first : first + PACKED] * kept
            halves.append(picked)
        packed[w] = jnp.concatenate(halves, axis=1)


def kernel(
    lsec, rsec, terms, psi, sub, lband, rband,
    applied_ref, vector_ref,
    l_out, r_out, l_in, r_in, psi_in, r_ready, mid, out, halo_in, rs_out, rs_in, app,
    mine, first_in, second_out, second_in,
    psi1_s, psi1_r, psi2_s, psi2_r, r1_s, r1_r, r2_s, r2_r, l1_s, l2_s, l_r, lt_s, lt_r,
    halo_s, halo_r, rs_s, rs_r, send_c, recv_c, send_d, recv_d,
):
    x = lax.axis_index("mpo")
    bond = lax.axis_index("bond")
    y = bond // 8
    q = lax.rem(bond, 8)
    z = q // 2
    c = lax.rem(q, 2)

    def device(dx, dy, dz, dc):
        return (dx, dy * 8 + dz * 2 + dc)

    def turn(value, step):
        return lax.rem(value + step + 4, 4)

    def remote(src, dst, send, recv, target):
        return pltpu.make_async_remote_copy(
            src_ref=src, dst_ref=dst, send_sem=send, recv_sem=recv,
            device_id=target, device_id_type=MESH,
        )

    def arrived(dst, send, recv):
        remote(dst, dst, send, recv, device(x, y, z, 1 - c)).wait_recv()

    def signal(target):
        pl.semaphore_signal(barrier, inc=1, device_id=target, device_id_type=MESH)

    l_self = (x == y) & (y == z)
    r_holder = c == x // 2
    r_self = (x == z) & r_holder
    low_edge = (z == 3) & (c == 1)
    high_edge = (z == 0) & (c == 0)

    barrier = pltpu.get_barrier_semaphore()
    for d in range(1, 8):
        other = lax.rem(q + d, 8)
        signal((x, y * 8 + other))
    for d in range(1, 16):
        other = lax.rem(x * 4 + y + d, 16)
        signal((other // 4, lax.rem(other, 4) * 8 + q))

    @pl.when(jnp.logical_not(l_self))
    def _():
        signal(device(z, x, y, c))

    for k in range(2):
        @pl.when(r_holder & jnp.logical_not((x == z) & (c == k)))
        def _(k=k):
            signal(device(z, y, x, k))

    @pl.when(x != y)
    def _():
        signal(device(y, x, z, 1 - c))

    @pl.when(z == 3)
    def _():
        signal(device(y, turn(x, -1), 3, 1))

    @pl.when(z == 0)
    def _():
        signal(device(y, turn(x, 1), 0, 0))

    @pl.when(c == 0)
    def _():
        signal(device(x, turn(y, -1), z, 1))

    @pl.when(c == 1)
    def _():
        signal(device(x, turn(y, 1), z, 0))

    expected = (
        23
        + as_int(jnp.logical_not(l_self))
        + as_int(jnp.logical_not((x == z) & (c == z // 2)))
        + as_int(x != y)
        + 2 * as_int(low_edge | high_edge)
    )
    pl.semaphore_wait(barrier, expected)

    def psi_rows(first):
        return psi_in.at[pl.ds(pl.multiple_of(first, 128), 128)]

    def psi_columns(k):
        return psi.at[:, pl.ds(pl.multiple_of(x * 1024 + k * 512, 512), 512)]

    own_rows = 128 + z * 256 + c * 128
    for k in range(2):
        here = (x == y) & (c == k)

        @pl.when(here)
        def _(k=k):
            pltpu.make_async_copy(psi_columns(k), psi_rows(own_rows), psi1_r.at[c]).start()

        @pl.when(jnp.logical_not(here))
        def _(k=k):
            remote(
                psi_columns(k), psi_rows(own_rows), psi1_s.at[k], psi1_r.at[c],
                device(y, x, z, k),
            ).start()

        @pl.when(low_edge)
        def _(k=k):
            remote(
                psi_columns(k), psi_rows(0), psi1_s.at[2 + k], psi1_r.at[2],
                device(turn(y, 1), x, 3, k),
            ).start()

        @pl.when(high_edge)
        def _(k=k):
            remote(
                psi_columns(k), psi_rows(1152), psi1_s.at[2 + k], psi1_r.at[2],
                device(turn(y, -1), x, 0, k),
            ).start()

    pack(rband, r_out, rsec, bond * 2, None)
    r_slot = r_in.at[lax.rem(z, 2) * 2 + c]

    @pl.when((x == z) & (c == z // 2))
    def _():
        pltpu.make_async_copy(r_out, r_slot, r1_r.at[c]).start()

    @pl.when(jnp.logical_not((x == z) & (c == z // 2)))
    def _():
        remote(r_out, r_slot, r1_s.at[0], r1_r.at[c], device(z, y, x, z // 2)).start()

    pack(lband, l_out, lsec, bond * 2, terms)
    l_slot = l_in.at[z * 2 + c]

    @pl.when(l_self)
    def _():
        pltpu.make_async_copy(l_out, l_slot, l_r.at[0]).start()

    @pl.when(jnp.logical_not(l_self))
    def _():
        remote(l_out, l_slot, l1_s.at[0], l_r.at[0], device(y, z, x, c)).start()

    for k in range(2):
        arrived(psi_rows(128 + z * 256 + k * 128), psi1_s.at[k], psi1_r.at[k])
    psi_block = psi_in.at[pl.ds(pl.multiple_of(128 + z * 256, 128), 256)]
    for d in range(1, 4):
        remote(
            psi_block, psi_block, psi2_s.at[d - 1], psi2_r.at[d - 1],
            device(x, y, turn(z, d), c),
        ).start()

    @pl.when(z == 3)
    def _():
        arrived(psi_rows(0), psi1_s.at[2], psi1_r.at[2])
        for d in range(1, 4):
            remote(
                psi_rows(0), psi_rows(0), psi2_s.at[2 + d], psi2_r.at[3],
                device(x, y, turn(z, d), c),
            ).start()

    @pl.when(z == 0)
    def _():
        arrived(psi_rows(1152), psi1_s.at[2], psi1_r.at[2])
        for d in range(1, 4):
            remote(
                psi_rows(1152), psi_rows(1152), psi2_s.at[2 + d], psi2_r.at[4],
                device(x, y, turn(z, d), c),
            ).start()

    r_first = lax.rem(x, 2) * 2
    r_pair = r_in.at[pl.ds(r_first, 2)]

    @pl.when(r_holder)
    def _():
        for k in range(2):
            arrived(r_in.at[r_first + k], r1_s.at[0], r1_r.at[k])
        for d in range(1, 4):
            remote(
                r_pair, r_pair, r2_s.at[d - 1], r2_r.at[lax.rem(x, 2)],
                device(turn(x, d), y, z, c),
            ).start()

    l_mine = l_in.at[y * 2 + c]
    arrived(l_mine, l1_s.at[0], l_r.at[0])
    for d in range(1, 4):
        remote(
            l_mine, l_mine, l2_s.at[d - 1], l_r.at[d], device(x, turn(y, d), z, c)
        ).start()

    mine[...] = jnp.zeros_like(mine)
    out[...] = jnp.zeros_like(out)
    gram_at = {}
    row = 5
    for k in range(4):
        for m in range(k, 4):
            gram_at[k, m] = row
            row += 1

    def gram(i, held):
        at = pl.ds(pl.multiple_of(i * 64, 64), 64)
        vectors = [sub[k, at, :].astype(jnp.float32) for k in range(4)]
        new = []
        for k in range(4):
            for m in range(k, 4):
                new.append(
                    held[len(new)]
                    + jnp.sum((vectors[k] * vectors[m]).reshape(8, 8, 128), axis=0)
                )
        return tuple(new)

    held = lax.fori_loop(
        0, 16, gram, tuple(jnp.zeros((8, 128), jnp.float32) for _ in range(10))
    )
    for k in range(10):
        mine[5 + k : 6 + k, :] = jnp.sum(held[k], axis=0, keepdims=True)

    for d in range(1, 4):
        other = turn(z, -d)
        block = psi_in.at[pl.ds(pl.multiple_of(128 + other * 256, 128), 256)]
        arrived(block, psi2_s.at[0], psi2_r.at[d - 1])

    @pl.when(z != 3)
    def _():
        arrived(psi_rows(0), psi2_s.at[0], psi2_r.at[3])

    @pl.when(z != 0)
    def _():
        arrived(psi_rows(1152), psi2_s.at[0], psi2_r.at[4])

    def left_shard(group, core):
        base = group * 4 + core * 2
        for h in range(2):
            p = place_in_sector(lsec, x * 16 + base + h)
            weights = [as_int(p == at).astype(jnp.float32) for at in range(SEC_MOST)]
            bands = l_in[group * 2 + core, :, :, h * PACKED : (h + 1) * PACKED].reshape(DEEP, PACKED)
            for n in range(2):
                source = 0.0
                for at in range(SEC_MOST):
                    first = pl.multiple_of((base + 2 + h - at) * TILE, TILE)
                    weight = jnp.zeros((1, 256), jnp.float32) + weights[at]
                    source = source + psi_in[
                        pl.ds(first, PACKED), n * 256 : (n + 1) * 256
                    ] * weight.astype(jnp.bfloat16)
                made = jnp.dot(bands, source, preferred_element_type=jnp.float32).astype(
                    jnp.bfloat16
                )
                rows = pl.ds(pl.multiple_of((base + h) * TILE, TILE), TILE)
                for w in range(TERMS):
                    mid[w, rows, n * 256 : (n + 1) * 256] = made[w * TILE : (w + 1) * TILE]

    def left_step(k, carry):
        d = k + k // 2 - 2 * (k // 3)
        group = turn(y, -d)
        own = l_in.at[group * 2 + c]
        twin = l_in.at[group * 2 + 1 - c]

        @pl.when(k > 0)
        def _():
            arrived(own, l1_s.at[0], l_r.at[d])

        remote(own, own, lt_s.at[d], lt_r.at[d], device(x, y, z, 1 - c)).start()
        left_shard(group, c)
        arrived(twin, l1_s.at[0], lt_r.at[d])
        left_shard(group, 1 - c)
        return carry

    lax.fori_loop(0, 4, left_step, 0)

    for k in range(2):
        @pl.when(x != 2 * c + k)
        def _(k=k):
            arrived(r_in.at[2 * k : 2 * k + 2], r2_s.at[0], r2_r.at[k])

    gap = jnp.zeros((DEEP, TILE), jnp.bfloat16)
    low = []
    for b in range(4):
        for h in range(2):
            p = place_in_sector(rsec, y * 16 + c * 8 + b * 2 + h)
            rows = r_in[b, :, :, h * PACKED : (h + 1) * PACKED].reshape(DEEP, PACKED)
            near = jnp.concatenate([rows, gap], axis=1)
            far = jnp.concatenate([gap, rows], axis=1)
            shifted = as_int((p == 1) if h == 0 else (p != 1))
            chosen = (jnp.zeros((1, 256), jnp.int32) + shifted).astype(jnp.bfloat16)
            r_ready[2 * b + h] = far * chosen + near * (1.0 - chosen)
            low.append(as_int((p >= 1) if h == 0 else (p == 2)).astype(jnp.float32))

    def right_block(g, b):
        rows = pl.ds(pl.multiple_of(g * 256, 256), 256)
        parts = [0.0, 0.0, 0.0]
        for h in range(2):
            j = 2 * b + h
            left = jnp.concatenate(
                [mid[w, rows, j * TILE : (j + 1) * TILE] for w in range(TERMS)], axis=1
            )
            made = jnp.dot(left, r_ready[j], preferred_element_type=jnp.float32)
            first, second = made[:, :128], made[:, 128:]
            parts[0] = parts[0] + low[j] * first
            parts[1] = parts[1] + (low[j] * second + (1.0 - low[j]) * first)
            parts[2] = parts[2] + (1.0 - low[j]) * second
        for i in range(3):
            out[rows, (b + i) * 128 : (b + i + 1) * 128] += parts[i]

    left_next = device(x, turn(y, -1 * as_int(c == 0)), z, 1 - c)
    right_next = device(x, turn(y, as_int(c == 1)), z, 1 - c)

    def outer_step(g, carry):
        rows = pl.ds(pl.multiple_of(g * 256, 256), 256)
        right_block(g, 0)
        right_block(g, 3)
        remote(
            out.at[rows, 0:128], halo_in.at[1, rows], halo_s.at[g], halo_r.at[4 + g], left_next
        ).start()
        remote(
            out.at[rows, 640:768], halo_in.at[0, rows], halo_s.at[4 + g], halo_r.at[g], right_next
        ).start()
        return carry

    lax.fori_loop(0, 4, outer_step, 0)

    def inner_step(g, carry):
        rows = pl.ds(pl.multiple_of(g * 256, 256), 256)
        right_block(g, 1)
        right_block(g, 2)
        for side in range(2):
            arrived(halo_in.at[side, rows], halo_s.at[0], halo_r.at[4 * side + g])
        for b in range(4):
            total = out[rows, (b + 1) * 128 : (b + 2) * 128]
            if b == 0:
                total = total + halo_in[0, rows]
            if b == 3:
                total = total + halo_in[1, rows]
            zt, ct = 2 * c + b // 2, b % 2
            here = (z == zt) & (c == ct)

            @pl.when(here)
            def _(total=total):
                rs_in[z, rows] = total.astype(jnp.bfloat16)

            @pl.when(jnp.logical_not(here))
            def _(total=total, b=b, zt=zt, ct=ct):
                rs_out[b, rows] = total.astype(jnp.bfloat16)
                remote(
                    rs_out.at[b, rows], rs_in.at[z, rows], rs_s.at[b * 4 + g], rs_r.at[z * 4 + g],
                    device(x, y, zt, ct),
                ).start()
        return carry

    lax.fori_loop(0, 4, inner_step, 0)

    def sums(i, held):
        rows = pl.ds(pl.multiple_of(i * 256, 256), 256)
        for zs in range(4):
            @pl.when(jnp.logical_not((z == zs) & (c == z // 2)))
            def _(zs=zs):
                arrived(rs_in.at[zs, rows], rs_s.at[0], rs_r.at[zs * 4 + i])
        block = (rs_in[0, rows].astype(jnp.float32) + rs_in[1, rows].astype(jnp.float32)) + (
            rs_in[2, rows].astype(jnp.float32) + rs_in[3, rows].astype(jnp.float32)
        )
        app[rows] = block
        new = [held[0] + jnp.sum((block * block).reshape(32, 8, 128), axis=0)]
        for k in range(4):
            product = sub[k, rows, :].astype(jnp.float32) * block
            new.append(held[k + 1] + jnp.sum(product.reshape(32, 8, 128), axis=0))
        return tuple(new)

    held = lax.fori_loop(0, 4, sums, tuple(jnp.zeros((8, 128), jnp.float32) for _ in range(5)))
    for k in range(5):
        mine[k : k + 1, :] = jnp.sum(held[k], axis=0, keepdims=True)

    copies = []
    for d in range(1, 8):
        copy = remote(
            mine, first_in.at[d - 1], send_c.at[d - 1], recv_c.at[d - 1],
            (x, y * 8 + lax.rem(q + d, 8)),
        )
        copy.start()
        copies.append(copy)
    for copy in copies:
        copy.wait()
    added = mine[...]
    for d in range(7):
        added = added + first_in[d]
    second_out[...] = added
    copies = []
    for d in range(1, 16):
        other = lax.rem(x * 4 + y + d, 16)
        copy = remote(
            second_out, second_in.at[d - 1], send_d.at[d - 1], recv_d.at[d - 1],
            (other // 4, lax.rem(other, 4) * 8 + q),
        )
        copy.start()
        copies.append(copy)
    for copy in copies:
        copy.wait()
    for d in range(15):
        added = added + second_in[d]
    sums_all = jnp.sum(added, axis=1, keepdims=True)

    def one(i):
        return sums_all[i : i + 1, :] * (1.0 / float(D_LEFT * D_RIGHT))

    coefficient = [one(1 + k) / (one(gram_at[k, k]) + epsilon) for k in range(4)]
    energy = one(0)
    for k in range(4):
        energy = energy - 2.0 * coefficient[k] * one(1 + k)
        for m in range(k, 4):
            twice = 1.0 if m == k else 2.0
            energy = energy + twice * coefficient[k] * coefficient[m] * one(gram_at[k, m])
    scale = lax.rsqrt(jnp.maximum(energy, 0.0) + epsilon)

    def write(i, carry):
        rows = pl.ds(pl.multiple_of(i * 128, 128), 128)
        block = app[rows]
        residual = block
        for k in range(4):
            residual = residual - coefficient[k] * sub[k, rows, :].astype(jnp.float32)
        applied_ref[rows, :] = block
        vector_ref[rows, :] = residual * scale
        return carry

    lax.fori_loop(0, 8, write, 0)

    def left(src, send):
        remote(src, src, send, l_r.at[0], device(x, y, z, 1 - c)).wait_send()

    for k in range(2):
        @pl.when(jnp.logical_not((x == y) & (c == k)))
        def _(k=k):
            left(psi_columns(k), psi1_s.at[k])

        @pl.when(low_edge | high_edge)
        def _(k=k):
            left(psi_columns(k), psi1_s.at[2 + k])

    @pl.when(jnp.logical_not((x == z) & (c == z // 2)))
    def _():
        left(r_out, r1_s.at[0])

    @pl.when(jnp.logical_not(l_self))
    def _():
        left(l_out, l1_s.at[0])

    for d in range(1, 4):
        left(psi_block, psi2_s.at[d - 1])
        left(l_mine, l2_s.at[d - 1])

        @pl.when((z == 3) | (z == 0))
        def _(d=d):
            left(psi_rows(0), psi2_s.at[2 + d])

        @pl.when(r_holder)
        def _(d=d):
            left(r_pair, r2_s.at[d - 1])

    for g in range(4):
        left(l_mine, lt_s.at[g])
        rows = slice(g * 256, (g + 1) * 256)
        left(out.at[rows, 0:128], halo_s.at[g])
        left(out.at[rows, 640:768], halo_s.at[4 + g])
        for b in range(4):
            zt, ct = 2 * c + b // 2, b % 2

            @pl.when(jnp.logical_not((z == zt) & (c == ct)))
            def _(b=b, rows=rows, g=g):
                left(rs_out.at[b, rows], rs_s.at[b * 4 + g])


def per_device(
    wavefunction, subspace, left_band, right_band, left_sector, right_sector, term_sectors
):
    shape = jax.ShapeDtypeStruct((1024, 128), jnp.float32)
    dma = pltpu.SemaphoreType.DMA
    bf16, f32 = jnp.bfloat16, jnp.float32
    vmem = pl.BlockSpec(memory_space=pltpu.VMEM)
    smem = pl.BlockSpec(memory_space=pltpu.SMEM)
    shard = (TERMS, TILE, 2 * PACKED)
    return pl.pallas_call(
        kernel,
        out_shape=(shape, shape),
        in_specs=[smem, smem, vmem, vmem, vmem, vmem, vmem],
        out_specs=(vmem, vmem),
        scratch_shapes=[
            pltpu.VMEM(shard, bf16),
            pltpu.VMEM(shard, bf16),
            pltpu.VMEM((8,) + shard, bf16),
            pltpu.VMEM((4,) + shard, bf16),
            pltpu.VMEM((1280, 512), bf16),
            pltpu.VMEM((8, DEEP, 256), bf16),
            pltpu.VMEM((TERMS, 1024, 512), bf16),
            pltpu.VMEM((1024, 768), f32),
            pltpu.VMEM((2, 1024, 128), f32),
            pltpu.VMEM((4, 1024, 128), bf16),
            pltpu.VMEM((4, 1024, 128), bf16),
            pltpu.VMEM((1024, 128), f32),
            pltpu.VMEM((16, 128), f32),
            pltpu.VMEM((7, 16, 128), f32),
            pltpu.VMEM((16, 128), f32),
            pltpu.VMEM((15, 16, 128), f32),
            dma((4,)), dma((3,)), dma((6,)), dma((5,)),
            dma((1,)), dma((2,)), dma((3,)), dma((2,)),
            dma((1,)), dma((3,)), dma((4,)), dma((4,)), dma((4,)),
            dma((8,)), dma((8,)), dma((16,)), dma((16,)),
            dma((7,)), dma((7,)), dma((15,)), dma((15,)),
        ],
        compiler_params=pltpu.CompilerParams(
            collective_id=0, has_side_effects=True, vmem_limit_bytes=56 * 1024 * 1024
        ),
        name="two_site_step",
    )(left_sector, right_sector, term_sectors, wavefunction, subspace, left_band, right_band)


def solution(mesh):
    return jax.shard_map(
        per_device,
        mesh=mesh,
        in_specs=(
            P("bond", None),
            P(None, "mpo", "bond"),
            P("mpo", "bond", None),
            P("mpo", "bond", None),
            P(),
            P(),
            P("mpo", None),
        ),
        out_specs=(P("mpo", "bond"), P("mpo", "bond")),
        check_vma=False,
    )
```

```python
import functools

import jax
import jax.numpy as jnp
from jax import lax
from jax.experimental import pallas as pl
from jax.experimental.pallas import tpu as pltpu
from jax.sharding import PartitionSpec as P

D_LEFT = 4096
D_RIGHT = 4096
TILE = 64
SEC_MOST = 3
PACKED = SEC_MOST * TILE
NT = 64
TERMS = 9
DEEP = TERMS * TILE
MESH = pl.DeviceIdType.MESH

epsilon = 1e-06


def as_int(flag):
    return flag.astype(jnp.int32)


def place_in_sector(sector, tile):
    here = sector[tile]
    one = as_int((tile >= 1) & (sector[jnp.maximum(tile - 1, 0)] == here))
    two = as_int((tile >= 2) & (sector[jnp.maximum(tile - 2, 0)] == here))
    return one + two


def sector_size(sector, tile):
    here = sector[tile]
    one = as_int((tile <= NT - 2) & (sector[jnp.minimum(tile + 1, NT - 1)] == here))
    two = as_int((tile <= NT - 3) & (sector[jnp.minimum(tile + 2, NT - 1)] == here))
    return 1 + place_in_sector(sector, tile) + one + two


def lanes_of(low, high):
    half = lax.broadcasted_iota(jnp.int32, (1, 128), 1) // TILE
    return low * (1 - half) + high * half


def pack_masks(sector, first_tile):
    row = lax.broadcasted_iota(jnp.int32, (PACKED, 128), 0)
    place = [place_in_sector(sector, first_tile + h) for h in range(2)]
    size = [sector_size(sector, first_tile + h) * TILE for h in range(2)]
    return [
        jnp.clip(
            lanes_of(size[0] * as_int(place[0] == at), size[1] * as_int(place[1] == at)) - row, 0, 1
        ).astype(jnp.bfloat16)
        for at in range(SEC_MOST)
    ]


def packed_term(band, w, masks):
    total = band[w, 2 * TILE : 2 * TILE + PACKED, :] * masks[0]
    total = total + band[w, TILE : TILE + PACKED, :] * masks[1]
    return total + band[w, :PACKED, :] * masks[2]


def kernel(
    lsec, rsec, terms, psi, sub, lband, rband,
    applied_ref, vector_ref,
    l_in, r_out, r_in, psi_in, r_wide, mid, out, halo_in, rs_out, rs_in, deal, app,
    mine, first_in, second_out, second_in,
    psi1_s, psi1_r, psi2_s, psi2_r, r_s, r_r, l_s, l_r, lt_s, lt_r,
    halo_s, halo_r, rs_s, rs_r, deal_s, deal_r, send_c, recv_c, send_d, recv_d,
):
    x = lax.axis_index("mpo")
    bond = lax.axis_index("bond")
    y = bond // 8
    q = lax.rem(bond, 8)
    z = q // 2
    c = lax.rem(q, 2)

    def device(dx, dy, dz, dc):
        return (dx, dy * 8 + dz * 2 + dc)

    def turn(value, step):
        return lax.rem(value + step + 4, 4)

    def remote(src, dst, send, recv, target):
        return pltpu.make_async_remote_copy(
            src_ref=src, dst_ref=dst, send_sem=send, recv_sem=recv,
            device_id=target, device_id_type=MESH,
        )

    twin = device(x, y, z, 1 - c)

    def arrived(dst, recv):
        remote(dst, dst, l_s.at[0], recv, twin).wait_recv()

    def left(src, send):
        remote(src, src, send, l_r.at[0], twin).wait_send()

    def signal(target):
        pl.semaphore_signal(barrier, inc=1, device_id=target, device_id_type=MESH)

    barrier = pltpu.get_barrier_semaphore()
    for d in range(1, 8):
        signal((x, y * 8 + lax.rem(q + d, 8)))
    for d in range(1, 16):
        other = lax.rem(x * 4 + y + d, 16)
        signal((other // 4, lax.rem(other, 4) * 8 + q))
    for d in range(1, 4):
        signal(device(x, turn(y, d), z, 1 - c))
        signal(device(x, turn(y, d), turn(z, -1), 1))
        signal(device(x, turn(y, d), turn(z, 1), 0))
    pl.semaphore_wait(barrier, 31)

    above = as_int((z == 3) & (c == 1))
    below = as_int((z == 0) & (c == 0))
    halo_y = turn(y, above - below)
    halo_z = turn(z, 2 * c - 1)
    halo_slot = 3 * (1 - c)
    own_rows = pl.ds(pl.multiple_of(x * 32, 32), 32)

    def psi_part(dy, k):
        return psi.at[own_rows, pl.ds(pl.multiple_of(dy * 1024 + k * 512, 512), 512)]

    for d in range(4):
        dy = turn(y, d)
        for k in range(2):
            n = 2 * d + k
            own = psi_in.at[y, 1 + c, x]
            if d == 0:
                @pl.when(c == k)
                def _(k=k, own=own, dy=dy):
                    pltpu.make_async_copy(psi_part(dy, k), own, psi1_r.at[y * 4 + 1 + c]).start()

                @pl.when(c != k)
                def _(k=k, own=own, dy=dy, n=n):
                    remote(
                        psi_part(dy, k), own, psi1_s.at[n], psi1_r.at[y * 4 + 1 + c],
                        device(x, dy, z, k),
                    ).start()
            else:
                remote(
                    psi_part(dy, k), own, psi1_s.at[n], psi1_r.at[y * 4 + 1 + c],
                    device(x, dy, z, k),
                ).start()
            remote(
                psi_part(dy, k), psi_in.at[halo_y, halo_slot, x], psi1_s.at[8 + n],
                psi1_r.at[halo_y * 4 + halo_slot], device(x, dy, halo_z, k),
            ).start()

    masks = pack_masks(lsec, bond * 2)
    number = lax.broadcasted_iota(jnp.int32, terms.shape, 1)
    active = []
    for h in range(2):
        same = 1 - jnp.clip(jnp.abs(number - lsec[bond * 2 + h]), 0, 1)
        active.append(jnp.sum(terms[...] * same, axis=1, keepdims=True))
    l_mine = l_in.at[y * 2 + c]
    for w in range(TERMS):
        switch = lanes_of(active[0][w : w + 1], active[1][w : w + 1]).astype(jnp.bfloat16)
        rows = (packed_term(lband, w, masks) * switch).T
        l_in[y * 2 + c, w] = jnp.concatenate([rows[:TILE], rows[TILE:]], axis=1)
    for d in range(1, 4):
        remote(l_mine, l_mine, l_s.at[d - 1], l_r.at[d], device(x, turn(y, d), z, c)).start()

    masks = pack_masks(rsec, bond * 2)
    for w in range(TERMS):
        r_out[w] = packed_term(rband, w, masks)
    r_slot = lax.rem(z, 2) * 2 + c

    @pl.when(c == z // 2)
    def _():
        pltpu.make_async_copy(r_out, r_in.at[r_slot], r_r.at[r_slot]).start()

    @pl.when(c != z // 2)
    def _():
        remote(r_out, r_in.at[r_slot], r_s.at[0], r_r.at[r_slot], twin).start()

    for d in range(1, 4):
        remote(
            r_out, r_in.at[r_slot], r_s.at[d], r_r.at[r_slot], device(x, y, turn(z, d), z // 2)
        ).start()

    order = [0, 1, 3, 2]
    for k in range(4):
        group = turn(y, -order[k])
        for slot in range(4):
            arrived(psi_in.at[group, slot, x], psi1_r.at[group * 4 + slot])
        part = psi_in.at[group, :, x]
        for d in range(1, 4):
            remote(
                part, part, psi2_s.at[3 * k + d - 1], psi2_r.at[4 * (d - 1) + group],
                device(turn(x, d), y, z, c),
            ).start()

    mine[...] = jnp.zeros_like(mine)
    out[...] = jnp.zeros_like(out)
    gram_at = {}
    row = 5
    for k in range(4):
        for m in range(k, 4):
            gram_at[k, m] = row
            row += 1

    def gram(i, held):
        at = pl.ds(pl.multiple_of(i * 64, 64), 64)
        vectors = [sub[k, at, :].astype(jnp.float32) for k in range(4)]
        new = []
        for k in range(4):
            for m in range(k, 4):
                new.append(
                    held[len(new)]
                    + jnp.sum((vectors[k] * vectors[m]).reshape(8, 8, 128), axis=0)
                )
        return tuple(new)

    held = lax.fori_loop(
        0, 16, gram, tuple(jnp.zeros((8, 128), jnp.float32) for _ in range(10))
    )
    for k in range(10):
        mine[5 + k : 6 + k, :] = jnp.sum(held[k], axis=0, keepdims=True)

    def left_shard(group, core):
        for h in range(2):
            p = place_in_sector(lsec, group * 16 + z * 4 + core * 2 + h)
            weights = [
                (jnp.zeros((1, 256), jnp.int32) + as_int(p == at)).astype(jnp.bfloat16)
                for at in range(SEC_MOST)
            ]
            bands = l_in[group * 2 + core, :, :, h * PACKED : (h + 1) * PACKED].reshape(DEEP, PACKED)
            first = 2 + core * 2 + h
            rows = pl.ds(pl.multiple_of(group * 256 + core * 128 + h * TILE, TILE), TILE)
            for n in range(2):
                lanes = slice(n * 256, (n + 1) * 256)
                tiles = {
                    t: jnp.concatenate(
                        [psi_in[group, t // 2, (t % 2) * 2 + i, :, lanes] for i in range(2)], axis=0
                    )
                    for t in range(first - 2, first + 3)
                }
                source = jnp.concatenate(
                    [
                        tiles[first + m] * weights[0]
                        + tiles[first + m - 1] * weights[1]
                        + tiles[first + m - 2] * weights[2]
                        for m in range(SEC_MOST)
                    ],
                    axis=0,
                )
                made = jnp.dot(bands, source, preferred_element_type=jnp.float32).astype(
                    jnp.bfloat16
                )
                for w in range(TERMS):
                    mid[w, rows, lanes] = made[w * TILE : (w + 1) * TILE]

    def left_step(k, carry):
        d = k + k // 2 - 2 * (k // 3)
        group = turn(y, -d)
        own = l_in.at[group * 2 + c]

        @pl.when(k > 0)
        def _():
            arrived(own, l_r.at[d])

        remote(own, own, lt_s.at[d], lt_r.at[d], twin).start()
        for e in range(1, 4):
            arrived(psi_in.at[group, :, turn(x, -e)], psi2_r.at[4 * (e - 1) + group])
        arrived(l_in.at[group * 2 + 1 - c], lt_r.at[d])
        left_shard(group, 0)
        left_shard(group, 1)
        return carry

    lax.fori_loop(0, 4, left_step, 0)

    for b in range(4):
        arrived(r_in.at[b], r_r.at[b])
        place = [place_in_sector(rsec, y * 16 + c * 8 + b * 2 + h) for h in range(2)]
        weights = {}
        for i in range(6):
            for m in range(SEC_MOST):
                weights[i, m] = lanes_of(
                    as_int(place[0] == m - i + 2), as_int(place[1] == m - i + 3)
                ).astype(jnp.bfloat16)
        for w in range(TERMS):
            parts = [r_in[b, w, m * TILE : (m + 1) * TILE, :] for m in range(SEC_MOST)]
            for i in range(6):
                total = None
                for m in range(SEC_MOST):
                    if 0 <= m - i + 3 <= 3:
                        term = parts[m] * weights[i, m]
                        total = term if total is None else total + term
                r_wide[b, i * TILE : (i + 1) * TILE, w * 128 : (w + 1) * 128] = total

    def right_block(g, b):
        rows = pl.ds(pl.multiple_of(g * 256, 256), 256)
        source = jnp.concatenate(
            [mid[w, rows, b * 128 : (b + 1) * 128] for w in range(TERMS)], axis=1
        )
        out[rows, b * 128 : b * 128 + 384] += lax.dot_general(
            source, r_wide[b], (((1,), (1,)), ((), ())), preferred_element_type=jnp.float32
        )

    left_next = device(x, turn(y, -1 * as_int(c == 0)), z, 1 - c)
    right_next = device(x, turn(y, as_int(c == 1)), z, 1 - c)

    def outer_step(i, carry):
        g = turn(x, i + 1)
        rows = pl.ds(pl.multiple_of(g * 256, 256), 256)
        right_block(g, 0)
        right_block(g, 3)
        remote(
            out.at[rows, 0:128], halo_in.at[1, rows], halo_s.at[i], halo_r.at[4 + i], left_next
        ).start()
        remote(
            out.at[rows, 640:768], halo_in.at[0, rows], halo_s.at[4 + i], halo_r.at[i], right_next
        ).start()
        return carry

    lax.fori_loop(0, 4, outer_step, 0)

    def columns_done(i, g):
        rows = pl.ds(pl.multiple_of(g * 256, 256), 256)
        right_block(g, 1)
        right_block(g, 2)
        for side in range(2):
            arrived(halo_in.at[side, rows], halo_r.at[4 * side + i])
        return [
            out[rows, 128:256] + halo_in[0, rows],
            out[rows, 256:384],
            out[rows, 384:512],
            out[rows, 512:640] + halo_in[1, rows],
        ]

    def inner_step(i, carry):
        g = turn(x, i + 1)
        for b, total in enumerate(columns_done(i, g)):
            rs_out[i, :, b * 128 : (b + 1) * 128] = total.astype(jnp.bfloat16)
        remote(rs_out.at[i], rs_in.at[i], rs_s.at[i], rs_r.at[i], device(g, y, z, c)).start()
        return carry

    lax.fori_loop(0, 3, inner_step, 0)
    kept = columns_done(3, x)
    for i in range(3):
        arrived(rs_in.at[i], rs_r.at[i])
    place_rows = pl.ds(pl.multiple_of(z * 256, 256), 256)
    for b in range(4):
        lanes = slice(b * 128, (b + 1) * 128)
        total = kept[b]
        for i in range(3):
            total = total + rs_in[i, :, lanes].astype(jnp.float32)
        zt, ct = 2 * c + b // 2, b % 2
        here = (z == zt) & (c == ct)

        @pl.when(here)
        def _(total=total):
            app[place_rows] = total

        @pl.when(jnp.logical_not(here))
        def _(total=total, b=b, zt=zt, ct=ct):
            deal[b] = total
            remote(
                deal.at[b], app.at[place_rows], deal_s.at[b], deal_r.at[z], device(x, y, zt, ct)
            ).start()

    def sums(i, held):
        rows = pl.ds(pl.multiple_of(i * 256, 256), 256)

        @pl.when(jnp.logical_not((z == i) & (c == z // 2)))
        def _():
            arrived(app.at[rows], deal_r.at[i])

        block = app[rows]
        new = [held[0] + jnp.sum((block * block).reshape(32, 8, 128), axis=0)]
        for k in range(4):
            product = sub[k, rows, :].astype(jnp.float32) * block
            new.append(held[k + 1] + jnp.sum(product.reshape(32, 8, 128), axis=0))
        return tuple(new)

    held = lax.fori_loop(0, 4, sums, tuple(jnp.zeros((8, 128), jnp.float32) for _ in range(5)))
    for k in range(5):
        mine[k : k + 1, :] = jnp.sum(held[k], axis=0, keepdims=True)

    copies = []
    for d in range(1, 8):
        copy = remote(
            mine, first_in.at[d - 1], send_c.at[d - 1], recv_c.at[d - 1],
            (x, y * 8 + lax.rem(q + d, 8)),
        )
        copy.start()
        copies.append(copy)
    for copy in copies:
        copy.wait()
    added = mine[...]
    for d in range(7):
        added = added + first_in[d]
    second_out[...] = added
    copies = []
    for d in range(1, 16):
        other = lax.rem(x * 4 + y + d, 16)
        copy = remote(
            second_out, second_in.at[d - 1], send_d.at[d - 1], recv_d.at[d - 1],
            (other // 4, lax.rem(other, 4) * 8 + q),
        )
        copy.start()
        copies.append(copy)
    for copy in copies:
        copy.wait()
    for d in range(15):
        added = added + second_in[d]
    sums_all = jnp.sum(added, axis=1, keepdims=True)

    def one(i):
        return sums_all[i : i + 1, :] * (1.0 / float(D_LEFT * D_RIGHT))

    coefficient = [one(1 + k) / (one(gram_at[k, k]) + epsilon) for k in range(4)]
    energy = one(0)
    for k in range(4):
        energy = energy - 2.0 * coefficient[k] * one(1 + k)
        for m in range(k, 4):
            twice = 1.0 if m == k else 2.0
            energy = energy + twice * coefficient[k] * coefficient[m] * one(gram_at[k, m])
    scale = lax.rsqrt(jnp.maximum(energy, 0.0) + epsilon)

    def write(i, carry):
        rows = pl.ds(pl.multiple_of(i * 128, 128), 128)
        block = app[rows]
        residual = block
        for k in range(4):
            residual = residual - coefficient[k] * sub[k, rows, :].astype(jnp.float32)
        applied_ref[rows, :] = block
        vector_ref[rows, :] = residual * scale
        return carry

    lax.fori_loop(0, 8, write, 0)

    for n in range(8):
        if n < 2:
            @pl.when(c != n)
            def _(n=n):
                left(psi_part(y, n), psi1_s.at[n])
        else:
            left(psi_part(y, 0), psi1_s.at[n])
        left(psi_part(y, 0), psi1_s.at[8 + n])

    @pl.when(c != z // 2)
    def _():
        left(r_out, r_s.at[0])

    for d in range(1, 4):
        left(r_out, r_s.at[d])
        left(l_mine, l_s.at[d - 1])
        left(rs_out.at[d - 1], rs_s.at[d - 1])
    for n in range(12):
        left(psi_in.at[0, :, x], psi2_s.at[n])
    for g in range(4):
        left(l_mine, lt_s.at[g])
        left(out.at[0:256, 0:128], halo_s.at[g])
        left(out.at[0:256, 640:768], halo_s.at[4 + g])
        zt, ct = 2 * c + g // 2, g % 2

        @pl.when(jnp.logical_not((z == zt) & (c == ct)))
        def _(g=g):
            left(deal.at[g], deal_s.at[g])


def per_device(
    wavefunction, subspace, left_band, right_band, left_sector, right_sector, term_sectors
):
    shape = jax.ShapeDtypeStruct((1024, 128), jnp.float32)
    dma = pltpu.SemaphoreType.DMA
    bf16, f32 = jnp.bfloat16, jnp.float32
    vmem = pl.BlockSpec(memory_space=pltpu.VMEM)
    smem = pl.BlockSpec(memory_space=pltpu.SMEM)
    return pl.pallas_call(
        kernel,
        out_shape=(shape, shape),
        in_specs=[smem, smem, vmem, vmem, vmem, vmem, vmem],
        out_specs=(vmem, vmem),
        scratch_shapes=[
            pltpu.VMEM((8, TERMS, TILE, 2 * PACKED), bf16),
            pltpu.VMEM((TERMS, PACKED, 128), bf16),
            pltpu.VMEM((4, TERMS, PACKED, 128), bf16),
            pltpu.VMEM((4, 4, 4, 32, 512), bf16),
            pltpu.VMEM((4, 384, TERMS * 128), bf16),
            pltpu.VMEM((TERMS, 1024, 512), bf16),
            pltpu.VMEM((1024, 768), f32),
            pltpu.VMEM((2, 1024, 128), f32),
            pltpu.VMEM((3, 256, 512), bf16),
            pltpu.VMEM((3, 256, 512), bf16),
            pltpu.VMEM((4, 256, 128), f32),
            pltpu.VMEM((1024, 128), f32),
            pltpu.VMEM((16, 128), f32),
            pltpu.VMEM((7, 16, 128), f32),
            pltpu.VMEM((16, 128), f32),
            pltpu.VMEM((15, 16, 128), f32),
            dma((16,)), dma((16,)), dma((12,)), dma((12,)),
            dma((4,)), dma((4,)), dma((3,)), dma((4,)), dma((4,)), dma((4,)),
            dma((8,)), dma((8,)), dma((3,)), dma((3,)), dma((4,)), dma((4,)),
            dma((7,)), dma((7,)), dma((15,)), dma((15,)),
        ],
        compiler_params=pltpu.CompilerParams(
            collective_id=0, has_side_effects=True, vmem_limit_bytes=56 * 1024 * 1024
        ),
        name="two_site_step",
    )(
        left_sector, right_sector, term_sectors, wavefunction, subspace,
        jnp.swapaxes(left_band, 1, 2), jnp.swapaxes(right_band, 1, 2),
    )


def solution(mesh):
    return jax.shard_map(
        per_device,
        mesh=mesh,
        in_specs=(
            P("bond", None),
            P(None, "mpo", "bond"),
            P("mpo", "bond", None),
            P("mpo", "bond", None),
            P(),
            P(),
            P("mpo", None),
        ),
        out_specs=(P("mpo", "bond"), P("mpo", "bond")),
        check_vma=False,
    )
```

```python
import functools

import jax
import jax.numpy as jnp
from jax import lax
from jax.experimental import pallas as pl
from jax.experimental.pallas import tpu as pltpu
from jax.sharding import PartitionSpec as P

D_LEFT = 4096
D_RIGHT = 4096
TILE = 64
SEC_MOST = 3
PACKED = SEC_MOST * TILE
NT = 64
TERMS = 9
DEEP = TERMS * TILE
MESH = pl.DeviceIdType.MESH

epsilon = 1e-06


def as_int(flag):
    return flag.astype(jnp.int32)


def place_in_sector(sector, tile):
    here = sector[tile]
    one = as_int((tile >= 1) & (sector[jnp.maximum(tile - 1, 0)] == here))
    two = as_int((tile >= 2) & (sector[jnp.maximum(tile - 2, 0)] == here))
    return one + two


def sector_size(sector, tile):
    here = sector[tile]
    one = as_int((tile <= NT - 2) & (sector[jnp.minimum(tile + 1, NT - 1)] == here))
    two = as_int((tile <= NT - 3) & (sector[jnp.minimum(tile + 2, NT - 1)] == here))
    return 1 + place_in_sector(sector, tile) + one + two


def lanes_of(low, high):
    half = lax.broadcasted_iota(jnp.int32, (1, 128), 1) // TILE
    return low * (1 - half) + high * half


def pack_masks(sector, first_tile):
    row = lax.broadcasted_iota(jnp.int32, (PACKED, 128), 0)
    place = [place_in_sector(sector, first_tile + h) for h in range(2)]
    size = [sector_size(sector, first_tile + h) * TILE for h in range(2)]
    return [
        jnp.clip(
            lanes_of(size[0] * as_int(place[0] == at), size[1] * as_int(place[1] == at)) - row, 0, 1
        ).astype(jnp.bfloat16)
        for at in range(SEC_MOST)
    ]


def packed_term(band, w, masks):
    total = band[w, 2 * TILE : 2 * TILE + PACKED, :] * masks[0]
    total = total + band[w, TILE : TILE + PACKED, :] * masks[1]
    return total + band[w, :PACKED, :] * masks[2]


def kernel(
    lsec, rsec, terms, psi, sub, lband, rband,
    applied_ref, vector_ref,
    l_in, r_out, r_in, psi_in, r_wide, mid, out, halo_out, halo_in, rs_out, rs_in, sub_in, deal, app,
    mine, first_in, second_out, second_in,
    psi1_s, psi1_r, psi2_s, psi2_r, r_s, r_r, rf_r, l_s, l_r, lt_s, lt_r,
    halo_s, halo_r, rs_s, rs_r, sub_s, sub_r, deal_s, deal_r, send_c, recv_c, send_d, recv_d,
):
    x = lax.axis_index("mpo")
    bond = lax.axis_index("bond")
    y = bond // 8
    q = lax.rem(bond, 8)
    z = q // 2
    c = lax.rem(q, 2)

    def device(dx, dy, dz, dc):
        return (dx, dy * 8 + dz * 2 + dc)

    def turn(value, step):
        return lax.rem(value + step + 4, 4)

    def remote(src, dst, send, recv, target):
        return pltpu.make_async_remote_copy(
            src_ref=src, dst_ref=dst, send_sem=send, recv_sem=recv,
            device_id=target, device_id_type=MESH,
        )

    twin = device(x, y, z, 1 - c)

    def arrived(dst, recv):
        remote(dst, dst, l_s.at[0], recv, twin).wait_recv()

    def left(src, send):
        remote(src, src, send, l_r.at[0], twin).wait_send()

    def signal(target):
        pl.semaphore_signal(barrier, inc=1, device_id=target, device_id_type=MESH)

    barrier = pltpu.get_barrier_semaphore()
    for d in range(1, 8):
        signal((x, y * 8 + lax.rem(q + d, 8)))
    for d in range(1, 16):
        other = lax.rem(x * 4 + y + d, 16)
        signal((other // 4, lax.rem(other, 4) * 8 + q))
    for d in range(1, 4):
        signal(device(x, turn(y, d), z, 1 - c))
        signal(device(x, turn(y, d), turn(z, -1), 1))
        signal(device(x, turn(y, d), turn(z, 1), 0))
    masks = pack_masks(lsec, bond * 2)
    number = lax.broadcasted_iota(jnp.int32, terms.shape, 1)
    active = []
    for h in range(2):
        same = 1 - jnp.clip(jnp.abs(number - lsec[bond * 2 + h]), 0, 1)
        active.append(jnp.sum(terms[...] * same, axis=1, keepdims=True))
    l_mine = l_in.at[y * 2 + c]
    for w in range(TERMS):
        switch = lanes_of(active[0][w : w + 1], active[1][w : w + 1]).astype(jnp.bfloat16)
        rows = (packed_term(lband, w, masks) * switch).T
        l_in[y * 2 + c, w] = jnp.concatenate([rows[:TILE], rows[TILE:]], axis=1)
    masks = pack_masks(rsec, bond * 2)
    for w in range(TERMS):
        r_out[w] = packed_term(rband, w, masks)
    mine[...] = jnp.zeros_like(mine)
    out[...] = jnp.zeros_like(out)
    pl.semaphore_wait(barrier, 31)

    above = as_int((z == 3) & (c == 1))
    below = as_int((z == 0) & (c == 0))
    halo_y = turn(y, above - below)
    halo_z = turn(z, 2 * c - 1)
    halo_slot = 3 * (1 - c)
    own_rows = pl.ds(pl.multiple_of(x * 32, 32), 32)

    def psi_part(dy, k):
        return psi.at[own_rows, pl.ds(pl.multiple_of(dy * 1024 + k * 512, 512), 512)]

    for d in range(4):
        dy = turn(y, d)
        for k in range(2):
            n = 2 * d + k
            own = psi_in.at[y, 1 + c, x]
            if d == 0:
                @pl.when(c == k)
                def _(k=k, own=own, dy=dy):
                    pltpu.make_async_copy(psi_part(dy, k), own, psi1_r.at[y * 4 + 1 + c]).start()

                @pl.when(c != k)
                def _(k=k, own=own, dy=dy, n=n):
                    remote(
                        psi_part(dy, k), own, psi1_s.at[n], psi1_r.at[y * 4 + 1 + c],
                        device(x, dy, z, k),
                    ).start()
            else:
                remote(
                    psi_part(dy, k), own, psi1_s.at[n], psi1_r.at[y * 4 + 1 + c],
                    device(x, dy, z, k),
                ).start()
            remote(
                psi_part(dy, k), psi_in.at[halo_y, halo_slot, x], psi1_s.at[8 + n],
                psi1_r.at[halo_y * 4 + halo_slot], device(x, dy, halo_z, k),
            ).start()

    remote(l_mine, l_mine, l_s.at[0], l_r.at[1], device(x, turn(y, 1), z, c)).start()
    remote(l_mine, l_mine, l_s.at[1], l_r.at[3], device(x, turn(y, -1), z, c)).start()
    remote(l_mine, l_mine, lt_s.at[0], lt_r.at[0], twin).start()

    r_slot = lax.rem(z, 2) * 2 + c

    @pl.when(c == z // 2)
    def _():
        pltpu.make_async_copy(r_out, r_in.at[r_slot], r_r.at[r_slot]).start()

    @pl.when(c != z // 2)
    def _():
        remote(r_out, r_in.at[r_slot], r_s.at[0], r_r.at[r_slot], twin).start()

    for n, d in enumerate((1, -1)):
        remote(
            r_out, r_in.at[r_slot], r_s.at[1 + n], r_r.at[r_slot], device(x, y, turn(z, d), z // 2)
        ).start()

    order = [0, 1, 3, 2]
    for k in range(4):
        group = turn(y, -order[k])
        for slot in range(4):
            arrived(psi_in.at[group, slot, x], psi1_r.at[group * 4 + slot])
        part = psi_in.at[group, :, x]
        for n, d in enumerate((1, -1)):
            remote(
                part, part, psi2_s.at[2 * k + n], psi2_r.at[4 * n + group],
                device(turn(x, d), y, z, c),
            ).start()

    def psi_further(k):
        d = k + k // 2 - 2 * (k // 3)
        group = turn(y, -d)
        for n, d in enumerate((1, -1)):
            arrived(psi_in.at[group, :, turn(x, -d)], psi2_r.at[4 * n + group])
            part = psi_in.at[group, 2 * n : 2 * n + 2, turn(x, -d)]
            remote(
                part, part, psi2_s.at[8 + 2 * k + n], psi2_r.at[8 + 4 * n + group],
                device(turn(x, d), y, z, c),
            ).start()

    def left_further():
        for n, d in enumerate((1, -1)):
            came = turn(y, -d) * 2 + c
            arrived(l_in.at[came], l_r.at[2 - d])
            remote(l_in.at[came], l_in.at[came], lt_s.at[2 - d], lt_r.at[2 - d], twin).start()
            part = l_in.at[came, :, 32 * n : 32 * n + 32]
            remote(
                part, part, l_s.at[2 + n], l_r.at[4 + n], device(x, turn(y, d), z, c)
            ).start()

    near = turn(z, (1 - 2 * lax.rem(z, 2)) * (1 - 2 * as_int(c != z // 2)))
    onward = turn(z, z - near)
    near_pair = lax.rem(near, 2) * 2
    half = as_int(onward != turn(z, 1))

    def right_part(first, which):
        return r_in.at[
            pl.ds(first, 2), :, pl.ds(pl.multiple_of(which * 96, 32), 96)
        ]

    def right_further():
        for n in range(2):
            arrived(r_in.at[near_pair + n], r_r.at[near_pair + n])
        part = right_part(near_pair, half)
        remote(part, part, r_s.at[3], rf_r.at[half], device(x, y, onward, c)).start()

    psi_further(0)
    psi_further(1)
    left_further()
    right_further()

    gram_at = {}
    row = 5
    for k in range(4):
        for m in range(k, 4):
            gram_at[k, m] = row
            row += 1

    def gram(i, held):
        at = pl.ds(pl.multiple_of(i * 64, 64), 64)
        vectors = [sub[k, at, :].astype(jnp.float32) for k in range(4)]
        new = []
        for k in range(4):
            for m in range(k, 4):
                new.append(
                    held[len(new)]
                    + jnp.sum((vectors[k] * vectors[m]).reshape(8, 8, 128), axis=0)
                )
        return tuple(new)

    held = lax.fori_loop(
        0, 16, gram, tuple(jnp.zeros((8, 128), jnp.float32) for _ in range(10))
    )
    for k in range(10):
        mine[5 + k : 6 + k, :] = jnp.sum(held[k], axis=0, keepdims=True)

    def left_shard(group, core):
        for h in range(2):
            p = place_in_sector(lsec, group * 16 + z * 4 + core * 2 + h)
            weights = [
                (jnp.zeros((1, 256), jnp.int32) + as_int(p == at)).astype(jnp.bfloat16)
                for at in range(SEC_MOST)
            ]
            bands = l_in[group * 2 + core, :, :, h * PACKED : (h + 1) * PACKED].reshape(DEEP, PACKED)
            first = 2 + core * 2 + h
            rows = pl.ds(pl.multiple_of(group * 256 + core * 128 + h * TILE, TILE), TILE)
            for n in range(2):
                lanes = slice(n * 256, (n + 1) * 256)
                tiles = {
                    t: jnp.concatenate(
                        [psi_in[group, t // 2, (t % 2) * 2 + i, :, lanes] for i in range(2)], axis=0
                    )
                    for t in range(first - 2, first + 3)
                }
                source = jnp.concatenate(
                    [
                        tiles[first + m] * weights[0]
                        + tiles[first + m - 1] * weights[1]
                        + tiles[first + m - 2] * weights[2]
                        for m in range(SEC_MOST)
                    ],
                    axis=0,
                )
                made = jnp.dot(bands, source, preferred_element_type=jnp.float32).astype(
                    jnp.bfloat16
                )
                for w in range(TERMS):
                    mid[w, rows, lanes] = made[w * TILE : (w + 1) * TILE]

    def left_step(k, carry):
        d = k + k // 2 - 2 * (k // 3)
        group = turn(y, -d)
        own = l_in.at[group * 2 + c]

        @pl.when(k < 2)
        def _():
            psi_further(k + 2)

        @pl.when(k == 3)
        def _():
            for n in range(2):
                arrived(l_in.at[group * 2 + c, :, 32 * n : 32 * n + 32], l_r.at[4 + n])
            remote(own, own, lt_s.at[d], lt_r.at[d], twin).start()

        for n in range(2):
            arrived(
                psi_in.at[group, 2 * n : 2 * n + 2, turn(x, 2)], psi2_r.at[8 + 4 * n + group]
            )
        arrived(l_in.at[group * 2 + 1 - c], lt_r.at[d])
        left_shard(group, 0)
        left_shard(group, 1)
        return carry

    lax.fori_loop(0, 4, left_step, 0)

    for d in range(4):
        zt = turn(z, d)
        part = sub.at[:, pl.ds(pl.multiple_of(zt * 256, 256), 256)]
        if d == 0:
            @pl.when(c == z // 2)
            def _(part=part):
                pltpu.make_async_copy(part, sub_in.at[r_slot], sub_r.at[r_slot]).start()

            @pl.when(c != z // 2)
            def _(part=part):
                remote(part, sub_in.at[r_slot], sub_s.at[0], sub_r.at[r_slot], twin).start()
        else:
            remote(
                part, sub_in.at[r_slot], sub_s.at[d], sub_r.at[r_slot], device(x, y, zt, z // 2)
            ).start()

    @pl.when(c == z // 2)
    def _():
        first = lax.rem(z, 2) * 2
        for n in range(2):
            arrived(r_in.at[first + n], r_r.at[first + n])

    @pl.when(c != z // 2)
    def _():
        for n in range(2):
            arrived(right_part(lax.rem(z, 2) * 2, n), rf_r.at[n])

    for b in range(4):
        place = [place_in_sector(rsec, y * 16 + c * 8 + b * 2 + h) for h in range(2)]
        weights = {}
        for i in range(6):
            for m in range(SEC_MOST):
                weights[i, m] = lanes_of(
                    as_int(place[0] == m - i + 2), as_int(place[1] == m - i + 3)
                ).astype(jnp.bfloat16)
        for w in range(TERMS):
            parts = [r_in[b, w, m * TILE : (m + 1) * TILE, :] for m in range(SEC_MOST)]
            for i in range(6):
                total = None
                for m in range(SEC_MOST):
                    if 0 <= m - i + 3 <= 3:
                        term = parts[m] * weights[i, m]
                        total = term if total is None else total + term
                r_wide[b, i * TILE : (i + 1) * TILE, w * 128 : (w + 1) * 128] = total

    def right_block(g, b):
        rows = pl.ds(pl.multiple_of(g * 256, 256), 256)
        source = jnp.concatenate(
            [mid[w, rows, b * 128 : (b + 1) * 128] for w in range(TERMS)], axis=1
        )
        out[rows, b * 128 : b * 128 + 384] += lax.dot_general(
            source, r_wide[b], (((1,), (1,)), ((), ())), preferred_element_type=jnp.float32
        )

    left_next = device(x, turn(y, -1 * as_int(c == 0)), z, 1 - c)
    right_next = device(x, turn(y, as_int(c == 1)), z, 1 - c)

    def outer_step(i, carry):
        g = turn(x, i + 1)
        rows = pl.ds(pl.multiple_of(g * 256, 256), 256)
        right_block(g, 0)
        right_block(g, 3)
        halo_out[0, rows] = out[rows, 0:128].astype(jnp.bfloat16)
        halo_out[1, rows] = out[rows, 640:768].astype(jnp.bfloat16)
        remote(
            halo_out.at[0, rows], halo_in.at[1, rows], halo_s.at[i], halo_r.at[4 + i], left_next
        ).start()
        remote(
            halo_out.at[1, rows], halo_in.at[0, rows], halo_s.at[4 + i], halo_r.at[i], right_next
        ).start()
        return carry

    lax.fori_loop(0, 4, outer_step, 0)

    def columns_done(i, g):
        rows = pl.ds(pl.multiple_of(g * 256, 256), 256)
        right_block(g, 1)
        right_block(g, 2)
        for side in range(2):
            arrived(halo_in.at[side, rows], halo_r.at[4 * side + i])
        return [
            out[rows, 128:256] + halo_in[0, rows].astype(jnp.float32),
            out[rows, 256:384],
            out[rows, 384:512],
            out[rows, 512:640] + halo_in[1, rows].astype(jnp.float32),
        ]

    def inner_step(i, carry):
        g = turn(x, i + 1)
        for b, total in enumerate(columns_done(i, g)):
            rs_out[i, :, b * 128 : (b + 1) * 128] = total.astype(jnp.bfloat16)
        remote(rs_out.at[i], rs_in.at[i], rs_s.at[i], rs_r.at[i], device(g, y, z, c)).start()
        return carry

    lax.fori_loop(0, 3, inner_step, 0)
    kept = columns_done(3, x)
    for i in range(3):
        arrived(rs_in.at[i], rs_r.at[i])
    place_rows = pl.ds(pl.multiple_of(z * 256, 256), 256)
    held = [jnp.zeros((8, 128), jnp.float32) for _ in range(5)]
    for b in range(4):
        lanes = slice(b * 128, (b + 1) * 128)
        total = kept[b]
        for i in range(3):
            total = total + rs_in[i, :, lanes].astype(jnp.float32)
        arrived(sub_in.at[b], sub_r.at[b])
        products = [total * total] + [
            sub_in[b, k].astype(jnp.float32) * total for k in range(4)
        ]
        for k in range(5):
            held[k] = held[k] + jnp.sum(products[k].reshape(32, 8, 128), axis=0)
        zt, ct = 2 * c + b // 2, b % 2
        here = (z == zt) & (c == ct)

        @pl.when(here)
        def _(total=total):
            app[place_rows] = total

        @pl.when(jnp.logical_not(here))
        def _(total=total, b=b, zt=zt, ct=ct):
            deal[b] = total
            remote(
                deal.at[b], app.at[place_rows], deal_s.at[b], deal_r.at[z], device(x, y, zt, ct)
            ).start()

    for k in range(5):
        mine[k : k + 1, :] = jnp.sum(held[k], axis=0, keepdims=True)

    copies = []
    for d in range(1, 8):
        copy = remote(
            mine, first_in.at[d - 1], send_c.at[d - 1], recv_c.at[d - 1],
            (x, y * 8 + lax.rem(q + d, 8)),
        )
        copy.start()
        copies.append(copy)
    for copy in copies:
        copy.wait()
    added = mine[...]
    for d in range(7):
        added = added + first_in[d]
    second_out[...] = added
    copies = []
    for d in range(1, 16):
        other = lax.rem(x * 4 + y + d, 16)
        copy = remote(
            second_out, second_in.at[d - 1], send_d.at[d - 1], recv_d.at[d - 1],
            (other // 4, lax.rem(other, 4) * 8 + q),
        )
        copy.start()
        copies.append(copy)
    for copy in copies:
        copy.wait()
    for d in range(15):
        added = added + second_in[d]
    sums_all = jnp.sum(added, axis=1, keepdims=True)

    def one(i):
        return sums_all[i : i + 1, :] * (1.0 / float(D_LEFT * D_RIGHT))

    coefficient = [one(1 + k) / (one(gram_at[k, k]) + epsilon) for k in range(4)]
    energy = one(0)
    for k in range(4):
        energy = energy - 2.0 * coefficient[k] * one(1 + k)
        for m in range(k, 4):
            twice = 1.0 if m == k else 2.0
            energy = energy + twice * coefficient[k] * coefficient[m] * one(gram_at[k, m])
    scale = lax.rsqrt(jnp.maximum(energy, 0.0) + epsilon)

    def write(i, carry):
        rows = pl.ds(pl.multiple_of(i * 128, 128), 128)
        block = app[rows]
        residual = block
        for k in range(4):
            residual = residual - coefficient[k] * sub[k, rows, :].astype(jnp.float32)
        applied_ref[rows, :] = block
        vector_ref[rows, :] = residual * scale
        return carry

    for i in range(4):
        @pl.when(jnp.logical_not((z == i) & (c == z // 2)))
        def _(i=i):
            arrived(app.at[i * 256 : (i + 1) * 256], deal_r.at[i])

    lax.fori_loop(0, 8, write, 0)

    for n in range(8):
        if n < 2:
            @pl.when(c != n)
            def _(n=n):
                left(psi_part(y, n), psi1_s.at[n])
        else:
            left(psi_part(y, 0), psi1_s.at[n])
        left(psi_part(y, 0), psi1_s.at[8 + n])

    @pl.when(c != z // 2)
    def _():
        left(r_out, r_s.at[0])
        left(sub.at[:, 0:256], sub_s.at[0])

    for d in range(1, 4):
        left(sub.at[:, 0:256], sub_s.at[d])
        left(rs_out.at[d - 1], rs_s.at[d - 1])
    for n in range(8):
        left(psi_in.at[0, :, x], psi2_s.at[n])
        left(psi_in.at[0, 0:2, x], psi2_s.at[8 + n])
    for n in range(2):
        left(l_mine, l_s.at[n])
        left(l_in.at[0, :, 0:32], l_s.at[2 + n])
        left(r_out, r_s.at[1 + n])
    left(right_part(near_pair, half), r_s.at[3])
    for g in range(4):
        left(l_mine, lt_s.at[g])
        left(halo_out.at[0, 0:256], halo_s.at[g])
        left(halo_out.at[1, 0:256], halo_s.at[4 + g])
        zt, ct = 2 * c + g // 2, g % 2

        @pl.when(jnp.logical_not((z == zt) & (c == ct)))
        def _(g=g):
            left(deal.at[g], deal_s.at[g])


def per_device(
    wavefunction, subspace, left_band, right_band, left_sector, right_sector, term_sectors
):
    shape = jax.ShapeDtypeStruct((1024, 128), jnp.float32)
    dma = pltpu.SemaphoreType.DMA
    bf16, f32 = jnp.bfloat16, jnp.float32
    vmem = pl.BlockSpec(memory_space=pltpu.VMEM)
    smem = pl.BlockSpec(memory_space=pltpu.SMEM)
    return pl.pallas_call(
        kernel,
        out_shape=(shape, shape),
        in_specs=[smem, smem, vmem, vmem, vmem, vmem, vmem],
        out_specs=(vmem, vmem),
        scratch_shapes=[
            pltpu.VMEM((8, TERMS, TILE, 2 * PACKED), bf16),
            pltpu.VMEM((TERMS, PACKED, 128), bf16),
            pltpu.VMEM((4, TERMS, PACKED, 128), bf16),
            pltpu.VMEM((4, 4, 4, 32, 512), bf16),
            pltpu.VMEM((4, 384, TERMS * 128), bf16),
            pltpu.VMEM((TERMS, 1024, 512), bf16),
            pltpu.VMEM((1024, 768), f32),
            pltpu.VMEM((2, 1024, 128), bf16),
            pltpu.VMEM((2, 1024, 128), bf16),
            pltpu.VMEM((3, 256, 512), bf16),
            pltpu.VMEM((3, 256, 512), bf16),
            pltpu.VMEM((4, 4, 256, 128), bf16),
            pltpu.VMEM((4, 256, 128), f32),
            pltpu.VMEM((1024, 128), f32),
            pltpu.VMEM((16, 128), f32),
            pltpu.VMEM((7, 16, 128), f32),
            pltpu.VMEM((16, 128), f32),
            pltpu.VMEM((15, 16, 128), f32),
            dma((16,)), dma((16,)), dma((16,)), dma((16,)),
            dma((4,)), dma((4,)), dma((2,)), dma((4,)), dma((6,)), dma((4,)), dma((4,)),
            dma((8,)), dma((8,)), dma((3,)), dma((3,)), dma((4,)), dma((4,)), dma((4,)), dma((4,)),
            dma((7,)), dma((7,)), dma((15,)), dma((15,)),
        ],
        compiler_params=pltpu.CompilerParams(
            collective_id=0, has_side_effects=True, vmem_limit_bytes=56 * 1024 * 1024
        ),
        name="two_site_step",
    )(
        left_sector, right_sector, term_sectors, wavefunction, subspace,
        jnp.swapaxes(left_band, 1, 2), jnp.swapaxes(right_band, 1, 2),
    )


def solution(mesh):
    return jax.shard_map(
        per_device,
        mesh=mesh,
        in_specs=(
            P("bond", None),
            P(None, "mpo", "bond"),
            P("mpo", "bond", None),
            P("mpo", "bond", None),
            P(),
            P(),
            P("mpo", None),
        ),
        out_specs=(P("mpo", "bond"), P("mpo", "bond")),
        check_vma=False,
    )
```

```python
import functools

import jax
import jax.numpy as jnp
from jax import lax
from jax.experimental import pallas as pl
from jax.experimental.pallas import tpu as pltpu
from jax.sharding import PartitionSpec as P

D_LEFT = 4096
D_RIGHT = 4096
TILE = 64
SEC_MOST = 3
PACKED = SEC_MOST * TILE
NT = 64
TERMS = 9
DEEP = TERMS * TILE
MESH = pl.DeviceIdType.MESH

epsilon = 1e-06


def as_int(flag):
    return flag.astype(jnp.int32)


def place_in_sector(sector, tile):
    here = sector[tile]
    one = as_int((tile >= 1) & (sector[jnp.maximum(tile - 1, 0)] == here))
    two = as_int((tile >= 2) & (sector[jnp.maximum(tile - 2, 0)] == here))
    return one + two


def sector_size(sector, tile):
    here = sector[tile]
    one = as_int((tile <= NT - 2) & (sector[jnp.minimum(tile + 1, NT - 1)] == here))
    two = as_int((tile <= NT - 3) & (sector[jnp.minimum(tile + 2, NT - 1)] == here))
    return 1 + place_in_sector(sector, tile) + one + two


def lanes_of(low, high):
    half = lax.broadcasted_iota(jnp.int32, (1, 128), 1) // TILE
    return low * (1 - half) + high * half


def pack_masks(sector, first_tile):
    row = lax.broadcasted_iota(jnp.int32, (PACKED, 128), 0)
    place = [place_in_sector(sector, first_tile + h) for h in range(2)]
    size = [sector_size(sector, first_tile + h) * TILE for h in range(2)]
    return [
        jnp.clip(
            lanes_of(size[0] * as_int(place[0] == at), size[1] * as_int(place[1] == at)) - row, 0, 1
        ).astype(jnp.bfloat16)
        for at in range(SEC_MOST)
    ]


def packed_term(band, w, masks):
    total = band[w, 2 * TILE : 2 * TILE + PACKED, :] * masks[0]
    total = total + band[w, TILE : TILE + PACKED, :] * masks[1]
    return total + band[w, :PACKED, :] * masks[2]


def kernel(
    lsec, rsec, terms, psi, sub, lband, rband,
    applied_ref, vector_ref,
    l_in, r_out, r_in, psi_in, r_wide, mid, out, halo_out, halo_in, rs_out, rs_in, sub_in, deal, app,
    mine, first_in, second_out, second_in,
    psi1_s, psi1_r, psi2_s, psi2_r, r_s, r_r, rf_r, l_s, l_r, lt_s, lt_r,
    halo_s, halo_r, rs_s, rs_r, sub_s, sub_r, deal_s, deal_r, send_c, recv_c, send_d, recv_d,
):
    x = lax.axis_index("mpo")
    bond = lax.axis_index("bond")
    y = bond // 8
    q = lax.rem(bond, 8)
    z = q // 2
    c = lax.rem(q, 2)

    def device(dx, dy, dz, dc):
        return (dx, dy * 8 + dz * 2 + dc)

    def turn(value, step):
        return lax.rem(value + step + 4, 4)

    def remote(src, dst, send, recv, target):
        return pltpu.make_async_remote_copy(
            src_ref=src, dst_ref=dst, send_sem=send, recv_sem=recv,
            device_id=target, device_id_type=MESH,
        )

    twin = device(x, y, z, 1 - c)

    def arrived(dst, recv):
        remote(dst, dst, l_s.at[0], recv, twin).wait_recv()

    def left(src, send):
        remote(src, src, send, l_r.at[0], twin).wait_send()

    def signal(target):
        pl.semaphore_signal(barrier, inc=1, device_id=target, device_id_type=MESH)

    barrier = pltpu.get_barrier_semaphore()
    for d in range(1, 8):
        signal((x, y * 8 + lax.rem(q + d, 8)))
    for d in range(1, 16):
        other = lax.rem(x * 4 + y + d, 16)
        signal((other // 4, lax.rem(other, 4) * 8 + q))
    for d in range(1, 4):
        signal(device(x, turn(y, d), z, 1 - c))
        signal(device(x, turn(y, d), turn(z, -1), 1))
        signal(device(x, turn(y, d), turn(z, 1), 0))
    masks = pack_masks(lsec, bond * 2)
    number = lax.broadcasted_iota(jnp.int32, terms.shape, 1)
    active = []
    for h in range(2):
        same = 1 - jnp.clip(jnp.abs(number - lsec[bond * 2 + h]), 0, 1)
        active.append(jnp.sum(terms[...] * same, axis=1, keepdims=True))
    l_mine = l_in.at[y * 2 + c]
    for w in range(TERMS):
        switch = lanes_of(active[0][w : w + 1], active[1][w : w + 1]).astype(jnp.bfloat16)
        rows = (packed_term(lband, w, masks) * switch).T
        l_in[y * 2 + c, w] = jnp.concatenate([rows[:TILE], rows[TILE:]], axis=1)
    masks = pack_masks(rsec, bond * 2)
    for w in range(TERMS):
        r_out[w] = packed_term(rband, w, masks)
    mine[...] = jnp.zeros_like(mine)
    out[...] = jnp.zeros_like(out)
    pl.semaphore_wait(barrier, 31)

    above = as_int((z == 3) & (c == 1))
    below = as_int((z == 0) & (c == 0))
    halo_y = turn(y, above - below)
    halo_z = turn(z, 2 * c - 1)
    halo_slot = 3 * (1 - c)
    own_rows = pl.ds(pl.multiple_of(x * 32, 32), 32)

    def psi_part(dy, k):
        return psi.at[own_rows, pl.ds(pl.multiple_of(dy * 1024 + k * 512, 512), 512)]

    for d in range(4):
        dy = turn(y, d)
        for k in range(2):
            n = 2 * d + k
            own = psi_in.at[y, 1 + c, x]
            if d == 0:
                @pl.when(c == k)
                def _(k=k, own=own, dy=dy):
                    pltpu.make_async_copy(psi_part(dy, k), own, psi1_r.at[y * 4 + 1 + c]).start()

                @pl.when(c != k)
                def _(k=k, own=own, dy=dy, n=n):
                    remote(
                        psi_part(dy, k), own, psi1_s.at[n], psi1_r.at[y * 4 + 1 + c],
                        device(x, dy, z, k),
                    ).start()
            else:
                remote(
                    psi_part(dy, k), own, psi1_s.at[n], psi1_r.at[y * 4 + 1 + c],
                    device(x, dy, z, k),
                ).start()
            remote(
                psi_part(dy, k), psi_in.at[halo_y, halo_slot, x], psi1_s.at[8 + n],
                psi1_r.at[halo_y * 4 + halo_slot], device(x, dy, halo_z, k),
            ).start()

    remote(l_mine, l_mine, l_s.at[0], l_r.at[1], device(x, turn(y, 1), z, c)).start()
    remote(l_mine, l_mine, l_s.at[1], l_r.at[3], device(x, turn(y, -1), z, c)).start()
    remote(l_mine, l_mine, lt_s.at[0], lt_r.at[0], twin).start()

    r_slot = lax.rem(z, 2) * 2 + c

    @pl.when(c == z // 2)
    def _():
        pltpu.make_async_copy(r_out, r_in.at[r_slot], r_r.at[r_slot]).start()

    @pl.when(c != z // 2)
    def _():
        remote(r_out, r_in.at[r_slot], r_s.at[0], r_r.at[r_slot], twin).start()

    for n, d in enumerate((1, -1)):
        remote(
            r_out, r_in.at[r_slot], r_s.at[1 + n], r_r.at[r_slot], device(x, y, turn(z, d), z // 2)
        ).start()

    order = [0, 1, 3, 2]
    for k in range(4):
        group = turn(y, -order[k])
        for slot in range(4):
            arrived(psi_in.at[group, slot, x], psi1_r.at[group * 4 + slot])
        part = psi_in.at[group, :, x]
        for n, d in enumerate((1, -1)):
            remote(
                part, part, psi2_s.at[2 * k + n], psi2_r.at[4 * n + group],
                device(turn(x, d), y, z, c),
            ).start()

    def psi_further(k):
        d = k + k // 2 - 2 * (k // 3)
        group = turn(y, -d)
        for n, d in enumerate((1, -1)):
            arrived(psi_in.at[group, :, turn(x, -d)], psi2_r.at[4 * n + group])
            part = psi_in.at[group, 2 * n : 2 * n + 2, turn(x, -d)]
            remote(
                part, part, psi2_s.at[8 + 2 * k + n], psi2_r.at[8 + 4 * n + group],
                device(turn(x, d), y, z, c),
            ).start()

    def left_further():
        for n, d in enumerate((1, -1)):
            came = turn(y, -d) * 2 + c
            arrived(l_in.at[came], l_r.at[2 - d])
            remote(l_in.at[came], l_in.at[came], lt_s.at[2 - d], lt_r.at[2 - d], twin).start()
            part = l_in.at[came, :, 32 * n : 32 * n + 32]
            remote(
                part, part, l_s.at[2 + n], l_r.at[4 + n], device(x, turn(y, d), z, c)
            ).start()

    near = turn(z, (1 - 2 * lax.rem(z, 2)) * (1 - 2 * as_int(c != z // 2)))
    onward = turn(z, z - near)
    near_pair = lax.rem(near, 2) * 2
    half = as_int(onward != turn(z, 1))

    def right_part(first, which):
        return r_in.at[
            pl.ds(first, 2), :, pl.ds(pl.multiple_of(which * 96, 32), 96)
        ]

    def right_further():
        for n in range(2):
            arrived(r_in.at[near_pair + n], r_r.at[near_pair + n])
        part = right_part(near_pair, half)
        remote(part, part, r_s.at[3], rf_r.at[half], device(x, y, onward, c)).start()

    psi_further(0)
    psi_further(1)
    left_further()
    right_further()

    gram_at = {}
    row = 5
    for k in range(4):
        for m in range(k, 4):
            gram_at[k, m] = row
            row += 1

    def gram(i, held):
        at = pl.ds(pl.multiple_of(i * 64, 64), 64)
        vectors = [sub[k, at, :].astype(jnp.float32) for k in range(4)]
        new = []
        for k in range(4):
            for m in range(k, 4):
                new.append(
                    held[len(new)]
                    + jnp.sum((vectors[k] * vectors[m]).reshape(8, 8, 128), axis=0)
                )
        return tuple(new)

    held = lax.fori_loop(
        0, 16, gram, tuple(jnp.zeros((8, 128), jnp.float32) for _ in range(10))
    )
    for k in range(10):
        mine[5 + k : 6 + k, :] = jnp.sum(held[k], axis=0, keepdims=True)

    def left_shard(group, core):
        for h in range(2):
            p = place_in_sector(lsec, group * 16 + z * 4 + core * 2 + h)
            weights = [
                (jnp.zeros((1, 256), jnp.int32) + as_int(p == at)).astype(jnp.bfloat16)
                for at in range(SEC_MOST)
            ]
            bands = l_in[group * 2 + core, :, :, h * PACKED : (h + 1) * PACKED].reshape(DEEP, PACKED)
            first = 2 + core * 2 + h
            rows = pl.ds(pl.multiple_of(group * 256 + core * 128 + h * TILE, TILE), TILE)
            for n in range(2):
                lanes = slice(n * 256, (n + 1) * 256)
                tiles = {
                    t: jnp.concatenate(
                        [psi_in[group, t // 2, (t % 2) * 2 + i, :, lanes] for i in range(2)], axis=0
                    )
                    for t in range(first - 2, first + 3)
                }
                source = jnp.concatenate(
                    [
                        tiles[first + m] * weights[0]
                        + tiles[first + m - 1] * weights[1]
                        + tiles[first + m - 2] * weights[2]
                        for m in range(SEC_MOST)
                    ],
                    axis=0,
                )
                made = jnp.dot(bands, source, preferred_element_type=jnp.float32).astype(
                    jnp.bfloat16
                )
                for w in range(TERMS):
                    mid[w, rows, lanes] = made[w * TILE : (w + 1) * TILE]

    def left_step(k, carry):
        d = k + k // 2 - 2 * (k // 3)
        group = turn(y, -d)
        own = l_in.at[group * 2 + c]

        @pl.when(k < 2)
        def _():
            psi_further(k + 2)

        @pl.when(k == 3)
        def _():
            for n in range(2):
                arrived(l_in.at[group * 2 + c, :, 32 * n : 32 * n + 32], l_r.at[4 + n])
            remote(own, own, lt_s.at[d], lt_r.at[d], twin).start()

        for n in range(2):
            arrived(
                psi_in.at[group, 2 * n : 2 * n + 2, turn(x, 2)], psi2_r.at[8 + 4 * n + group]
            )
        arrived(l_in.at[group * 2 + 1 - c], lt_r.at[d])
        left_shard(group, 0)
        left_shard(group, 1)
        return carry

    lax.fori_loop(0, 4, left_step, 0)

    for d in range(4):
        zt = turn(z, d)
        part = sub.at[:, pl.ds(pl.multiple_of(zt * 256, 256), 256)]
        if d == 0:
            @pl.when(c == z // 2)
            def _(part=part):
                pltpu.make_async_copy(part, sub_in.at[r_slot], sub_r.at[r_slot]).start()

            @pl.when(c != z // 2)
            def _(part=part):
                remote(part, sub_in.at[r_slot], sub_s.at[0], sub_r.at[r_slot], twin).start()
        else:
            remote(
                part, sub_in.at[r_slot], sub_s.at[d], sub_r.at[r_slot], device(x, y, zt, z // 2)
            ).start()

    @pl.when(c == z // 2)
    def _():
        first = lax.rem(z, 2) * 2
        for n in range(2):
            arrived(r_in.at[first + n], r_r.at[first + n])

    @pl.when(c != z // 2)
    def _():
        for n in range(2):
            arrived(right_part(lax.rem(z, 2) * 2, n), rf_r.at[n])

    for b in range(4):
        place = [place_in_sector(rsec, y * 16 + c * 8 + b * 2 + h) for h in range(2)]
        weights = {}
        for i in range(6):
            for m in range(SEC_MOST):
                weights[i, m] = lanes_of(
                    as_int(place[0] == m - i + 2), as_int(place[1] == m - i + 3)
                ).astype(jnp.bfloat16)
        for w in range(TERMS):
            parts = [r_in[b, w, m * TILE : (m + 1) * TILE, :] for m in range(SEC_MOST)]
            for i in range(6):
                total = None
                for m in range(SEC_MOST):
                    if 0 <= m - i + 3 <= 3:
                        term = parts[m] * weights[i, m]
                        total = term if total is None else total + term
                r_wide[b, i * TILE : (i + 1) * TILE, w * 128 : (w + 1) * 128] = total

    def right_block(g, b):
        rows = pl.ds(pl.multiple_of(g * 256, 256), 256)
        source = jnp.concatenate(
            [mid[w, rows, b * 128 : (b + 1) * 128] for w in range(TERMS)], axis=1
        )
        out[rows, b * 128 : b * 128 + 384] += lax.dot_general(
            source, r_wide[b], (((1,), (1,)), ((), ())), preferred_element_type=jnp.float32
        )

    left_next = device(x, turn(y, -1 * as_int(c == 0)), z, 1 - c)
    right_next = device(x, turn(y, as_int(c == 1)), z, 1 - c)

    def right_step(i, carry):
        g = turn(x, i + 1)
        rows = pl.ds(pl.multiple_of(g * 256, 256), 256)
        right_block(g, 0)
        right_block(g, 3)
        halo_out[0, rows] = out[rows, 0:128].astype(jnp.bfloat16)
        halo_out[1, rows] = out[rows, 640:768].astype(jnp.bfloat16)
        remote(
            halo_out.at[0, rows], halo_in.at[1, rows], halo_s.at[i], halo_r.at[4 + i], left_next
        ).start()
        remote(
            halo_out.at[1, rows], halo_in.at[0, rows], halo_s.at[4 + i], halo_r.at[i], right_next
        ).start()
        right_block(g, 1)
        right_block(g, 2)

        @pl.when(i < 3)
        def _():
            rs_out[0, i] = out[rows, 256:512].astype(jnp.bfloat16)
            remote(
                rs_out.at[0, i], rs_in.at[0, i], rs_s.at[i], rs_r.at[i], device(g, y, z, c)
            ).start()

        return carry

    lax.fori_loop(0, 4, right_step, 0)

    def edge_columns(i, g):
        rows = pl.ds(pl.multiple_of(g * 256, 256), 256)
        for side in range(2):
            arrived(halo_in.at[side, rows], halo_r.at[4 * side + i])
        return (
            out[rows, 128:256] + halo_in[0, rows].astype(jnp.float32),
            out[rows, 512:640] + halo_in[1, rows].astype(jnp.float32),
        )

    def edge_step(i, carry):
        g = turn(x, i + 1)
        for n, total in enumerate(edge_columns(i, g)):
            rs_out[1, i, :, n * 128 : (n + 1) * 128] = total.astype(jnp.bfloat16)
        remote(
            rs_out.at[1, i], rs_in.at[1, i], rs_s.at[3 + i], rs_r.at[3 + i], device(g, y, z, c)
        ).start()
        return carry

    lax.fori_loop(0, 3, edge_step, 0)

    own_group = pl.ds(pl.multiple_of(x * 256, 256), 256)
    place_rows = pl.ds(pl.multiple_of(z * 256, 256), 256)
    held = [jnp.zeros((8, 128), jnp.float32) for _ in range(5)]
    for turn_of in range(2):
        if turn_of == 0:
            kept = (out[own_group, 256:384], out[own_group, 384:512])
        else:
            kept = edge_columns(3, x)
        for i in range(3):
            arrived(rs_in.at[turn_of, i], rs_r.at[3 * turn_of + i])
        for n in range(2):
            b = (1 + n) if turn_of == 0 else 3 * n
            total = kept[n]
            for i in range(3):
                total = total + rs_in[turn_of, i, :, n * 128 : (n + 1) * 128].astype(jnp.float32)
            zt, ct = 2 * c + b // 2, b % 2
            here = (z == zt) & (c == ct)

            @pl.when(here)
            def _(total=total):
                app[place_rows] = total

            @pl.when(jnp.logical_not(here))
            def _(total=total, b=b, zt=zt, ct=ct):
                deal[b] = total
                remote(
                    deal.at[b], app.at[place_rows], deal_s.at[b], deal_r.at[z],
                    device(x, y, zt, ct),
                ).start()

            arrived(sub_in.at[b], sub_r.at[b])
            products = [total * total] + [
                sub_in[b, k].astype(jnp.float32) * total for k in range(4)
            ]
            for k in range(5):
                held[k] = held[k] + jnp.sum(products[k].reshape(32, 8, 128), axis=0)
    for k in range(5):
        mine[k : k + 1, :] = jnp.sum(held[k], axis=0, keepdims=True)

    copies = []
    for d in range(1, 16):
        other = lax.rem(x * 4 + y + d, 16)
        copy = remote(
            mine, first_in.at[d - 1], send_c.at[d - 1], recv_c.at[d - 1],
            (other // 4, lax.rem(other, 4) * 8 + q),
        )
        copy.start()
        copies.append(copy)
    for copy in copies:
        copy.wait()
    added = mine[...]
    for d in range(15):
        added = added + first_in[d]
    second_out[...] = added
    copies = []
    for d in range(1, 8):
        copy = remote(
            second_out, second_in.at[d - 1], send_d.at[d - 1], recv_d.at[d - 1],
            (x, y * 8 + lax.rem(q + d, 8)),
        )
        copy.start()
        copies.append(copy)
    for copy in copies:
        copy.wait()
    for d in range(7):
        added = added + second_in[d]
    sums_all = jnp.sum(added, axis=1, keepdims=True)

    def one(i):
        return sums_all[i : i + 1, :] * (1.0 / float(D_LEFT * D_RIGHT))

    coefficient = [one(1 + k) / (one(gram_at[k, k]) + epsilon) for k in range(4)]
    energy = one(0)
    for k in range(4):
        energy = energy - 2.0 * coefficient[k] * one(1 + k)
        for m in range(k, 4):
            twice = 1.0 if m == k else 2.0
            energy = energy + twice * coefficient[k] * coefficient[m] * one(gram_at[k, m])
    scale = lax.rsqrt(jnp.maximum(energy, 0.0) + epsilon)

    def write(i, carry):
        rows = pl.ds(pl.multiple_of(i * 128, 128), 128)
        block = app[rows]
        residual = block
        for k in range(4):
            residual = residual - coefficient[k] * sub[k, rows, :].astype(jnp.float32)
        applied_ref[rows, :] = block
        vector_ref[rows, :] = residual * scale
        return carry

    for i in range(4):
        @pl.when(jnp.logical_not((z == i) & (c == z // 2)))
        def _(i=i):
            arrived(app.at[i * 256 : (i + 1) * 256], deal_r.at[i])

    lax.fori_loop(0, 8, write, 0)

    for n in range(8):
        if n < 2:
            @pl.when(c != n)
            def _(n=n):
                left(psi_part(y, n), psi1_s.at[n])
        else:
            left(psi_part(y, 0), psi1_s.at[n])
        left(psi_part(y, 0), psi1_s.at[8 + n])

    @pl.when(c != z // 2)
    def _():
        left(r_out, r_s.at[0])
        left(sub.at[:, 0:256], sub_s.at[0])

    for d in range(1, 4):
        left(sub.at[:, 0:256], sub_s.at[d])
        left(rs_out.at[0, d - 1], rs_s.at[d - 1])
        left(rs_out.at[1, d - 1], rs_s.at[2 + d])
    for n in range(8):
        left(psi_in.at[0, :, x], psi2_s.at[n])
        left(psi_in.at[0, 0:2, x], psi2_s.at[8 + n])
    for n in range(2):
        left(l_mine, l_s.at[n])
        left(l_in.at[0, :, 0:32], l_s.at[2 + n])
        left(r_out, r_s.at[1 + n])
    left(right_part(near_pair, half), r_s.at[3])
    for g in range(4):
        left(l_mine, lt_s.at[g])
        left(halo_out.at[0, 0:256], halo_s.at[g])
        left(halo_out.at[1, 0:256], halo_s.at[4 + g])
        zt, ct = 2 * c + g // 2, g % 2

        @pl.when(jnp.logical_not((z == zt) & (c == ct)))
        def _(g=g):
            left(deal.at[g], deal_s.at[g])


def per_device(
    wavefunction, subspace, left_band, right_band, left_sector, right_sector, term_sectors
):
    shape = jax.ShapeDtypeStruct((1024, 128), jnp.float32)
    dma = pltpu.SemaphoreType.DMA
    bf16, f32 = jnp.bfloat16, jnp.float32
    vmem = pl.BlockSpec(memory_space=pltpu.VMEM)
    smem = pl.BlockSpec(memory_space=pltpu.SMEM)
    return pl.pallas_call(
        kernel,
        out_shape=(shape, shape),
        in_specs=[smem, smem, vmem, vmem, vmem, vmem, vmem],
        out_specs=(vmem, vmem),
        scratch_shapes=[
            pltpu.VMEM((8, TERMS, TILE, 2 * PACKED), bf16),
            pltpu.VMEM((TERMS, PACKED, 128), bf16),
            pltpu.VMEM((4, TERMS, PACKED, 128), bf16),
            pltpu.VMEM((4, 4, 4, 32, 512), bf16),
            pltpu.VMEM((4, 384, TERMS * 128), bf16),
            pltpu.VMEM((TERMS, 1024, 512), bf16),
            pltpu.VMEM((1024, 768), f32),
            pltpu.VMEM((2, 1024, 128), bf16),
            pltpu.VMEM((2, 1024, 128), bf16),
            pltpu.VMEM((2, 3, 256, 256), bf16),
            pltpu.VMEM((2, 3, 256, 256), bf16),
            pltpu.VMEM((4, 4, 256, 128), bf16),
            pltpu.VMEM((4, 256, 128), f32),
            pltpu.VMEM((1024, 128), f32),
            pltpu.VMEM((16, 128), f32),
            pltpu.VMEM((15, 16, 128), f32),
            pltpu.VMEM((16, 128), f32),
            pltpu.VMEM((7, 16, 128), f32),
            dma((16,)), dma((16,)), dma((16,)), dma((16,)),
            dma((4,)), dma((4,)), dma((2,)), dma((4,)), dma((6,)), dma((4,)), dma((4,)),
            dma((8,)), dma((8,)), dma((6,)), dma((6,)), dma((4,)), dma((4,)), dma((4,)), dma((4,)),
            dma((15,)), dma((15,)), dma((7,)), dma((7,)),
        ],
        compiler_params=pltpu.CompilerParams(
            collective_id=0, has_side_effects=True, vmem_limit_bytes=56 * 1024 * 1024
        ),
        name="two_site_step",
    )(
        left_sector, right_sector, term_sectors, wavefunction, subspace,
        jnp.swapaxes(left_band, 1, 2), jnp.swapaxes(right_band, 1, 2),
    )


def solution(mesh):
    return jax.shard_map(
        per_device,
        mesh=mesh,
        in_specs=(
            P("bond", None),
            P(None, "mpo", "bond"),
            P("mpo", "bond", None),
            P("mpo", "bond", None),
            P(),
            P(),
            P("mpo", None),
        ),
        out_specs=(P("mpo", "bond"), P("mpo", "bond")),
        check_vma=False,
    )
```

```python
import functools

import jax
import jax.numpy as jnp
from jax import lax
from jax.experimental import pallas as pl
from jax.experimental.pallas import tpu as pltpu
from jax.sharding import PartitionSpec as P

D_LEFT = 4096
D_RIGHT = 4096
TILE = 64
SEC_MOST = 3
PACKED = SEC_MOST * TILE
NT = 64
TERMS = 9
DEEP = TERMS * TILE
MESH = pl.DeviceIdType.MESH

epsilon = 1e-06


def as_int(flag):
    return flag.astype(jnp.int32)


def place_in_sector(sector, tile):
    here = sector[tile]
    one = as_int((tile >= 1) & (sector[jnp.maximum(tile - 1, 0)] == here))
    two = as_int((tile >= 2) & (sector[jnp.maximum(tile - 2, 0)] == here))
    return one + two


def sector_size(sector, tile):
    here = sector[tile]
    one = as_int((tile <= NT - 2) & (sector[jnp.minimum(tile + 1, NT - 1)] == here))
    two = as_int((tile <= NT - 3) & (sector[jnp.minimum(tile + 2, NT - 1)] == here))
    return 1 + place_in_sector(sector, tile) + one + two


def lanes_of(low, high):
    half = lax.broadcasted_iota(jnp.int32, (1, 128), 1) // TILE
    return low * (1 - half) + high * half


def pack_masks(sector, first_tile):
    row = lax.broadcasted_iota(jnp.int32, (PACKED, 128), 0)
    place = [place_in_sector(sector, first_tile + h) for h in range(2)]
    size = [sector_size(sector, first_tile + h) * TILE for h in range(2)]
    return [
        jnp.clip(
            lanes_of(size[0] * as_int(place[0] == at), size[1] * as_int(place[1] == at)) - row, 0, 1
        ).astype(jnp.bfloat16)
        for at in range(SEC_MOST)
    ]


def packed_term(band, w, masks):
    total = band[w, 2 * TILE : 2 * TILE + PACKED, :] * masks[0]
    total = total + band[w, TILE : TILE + PACKED, :] * masks[1]
    return total + band[w, :PACKED, :] * masks[2]


def kernel(
    lsec, rsec, terms, psi, sub, lband, rband,
    applied_ref, vector_ref,
    l_in, r_out, r_in, psi_in, r_wide, mid, out, halo_out, halo_in, rs_out, rs_in, sub_in, deal, app,
    mine, folded, first_in, second_out, second_in,
    psi1_s, psi1_r, psi2_s, psi2_r, r_s, r_r, rf_r, l_s, l_r, lt_s, lt_r,
    halo_s, halo_r, rs_s, rs_r, sub_s, sub_r, deal_s, deal_r, send_c, recv_c, send_d, recv_d,
):
    x = lax.axis_index("mpo")
    bond = lax.axis_index("bond")
    y = bond // 8
    q = lax.rem(bond, 8)
    z = q // 2
    c = lax.rem(q, 2)

    def device(dx, dy, dz, dc):
        return (dx, dy * 8 + dz * 2 + dc)

    def turn(value, step):
        return lax.rem(value + step + 4, 4)

    def remote(src, dst, send, recv, target):
        return pltpu.make_async_remote_copy(
            src_ref=src, dst_ref=dst, send_sem=send, recv_sem=recv,
            device_id=target, device_id_type=MESH,
        )

    twin = device(x, y, z, 1 - c)

    def arrived(dst, recv):
        remote(dst, dst, l_s.at[0], recv, twin).wait_recv()

    def left(src, send):
        remote(src, src, send, l_r.at[0], twin).wait_send()

    def signal(target):
        pl.semaphore_signal(barrier, inc=1, device_id=target, device_id_type=MESH)

    barrier = pltpu.get_barrier_semaphore()
    for d in range(1, 8):
        signal((x, y * 8 + lax.rem(q + d, 8)))
    for d in range(1, 16):
        other = lax.rem(x * 4 + y + d, 16)
        signal((other // 4, lax.rem(other, 4) * 8 + q))
    for d in range(1, 4):
        signal(device(x, turn(y, d), z, 1 - c))
        signal(device(x, turn(y, d), turn(z, -1), 1))
        signal(device(x, turn(y, d), turn(z, 1), 0))
    masks = pack_masks(lsec, bond * 2)
    number = lax.broadcasted_iota(jnp.int32, terms.shape, 1)
    active = []
    for h in range(2):
        same = 1 - jnp.clip(jnp.abs(number - lsec[bond * 2 + h]), 0, 1)
        active.append(jnp.sum(terms[...] * same, axis=1, keepdims=True))
    l_mine = l_in.at[y * 2 + c]
    for w in range(TERMS):
        switch = lanes_of(active[0][w : w + 1], active[1][w : w + 1]).astype(jnp.bfloat16)
        rows = (packed_term(lband, w, masks) * switch).T
        l_in[y * 2 + c, w] = jnp.concatenate([rows[:TILE], rows[TILE:]], axis=1)
    masks = pack_masks(rsec, bond * 2)
    for w in range(TERMS):
        r_out[w] = packed_term(rband, w, masks)
    mine[...] = jnp.zeros_like(mine)
    out[...] = jnp.zeros_like(out)
    pl.semaphore_wait(barrier, 31)

    above = as_int((z == 3) & (c == 1))
    below = as_int((z == 0) & (c == 0))
    halo_y = turn(y, above - below)
    halo_z = turn(z, 2 * c - 1)
    halo_slot = 3 * (1 - c)
    own_rows = pl.ds(pl.multiple_of(x * 32, 32), 32)

    def psi_columns(dy, k):
        return pl.ds(pl.multiple_of(dy * 1024 + k * 512, 512), 512)

    def psi_part(dy, k):
        return psi.at[own_rows, psi_columns(dy, k)]

    def psi_whole(dy, k):
        return psi.at[:, psi_columns(dy, k)]

    def psi_quarter(group, slot, part):
        return psi_in.at[group, slot, pl.ds(pl.multiple_of(part * 32, 32), 32)]

    for k in range(2):
        @pl.when(c == k)
        def _(k=k):
            pltpu.make_async_copy(
                psi_whole(y, k), psi_in.at[y, 1 + c], psi1_r.at[y * 4 + 1 + c]
            ).start()

        @pl.when(c != k)
        def _(k=k):
            remote(
                psi_whole(y, k), psi_in.at[y, 1 + c], psi1_s.at[k], psi1_r.at[y * 4 + 1 + c], twin
            ).start()

    for d in (1, 3, 2, 0):
        dy = turn(y, d)
        hy = turn(halo_y, d)
        for k in range(2):
            n = 2 * d + k
            if d > 0:
                remote(
                    psi_part(dy, k), psi_quarter(y, 1 + c, x), psi1_s.at[n],
                    psi1_r.at[y * 4 + 1 + c], device(x, dy, z, k),
                ).start()
                source, target = psi_part(hy, k), psi_quarter(halo_y, halo_slot, x)
            else:
                source, target = psi_whole(hy, k), psi_in.at[halo_y, halo_slot]
            remote(
                source, target, psi1_s.at[8 + n], psi1_r.at[halo_y * 4 + halo_slot],
                device(x, hy, halo_z, k),
            ).start()

    remote(l_mine, l_mine, l_s.at[0], l_r.at[1], device(x, turn(y, 1), z, c)).start()
    remote(l_mine, l_mine, l_s.at[1], l_r.at[3], device(x, turn(y, -1), z, c)).start()
    remote(l_mine, l_mine, lt_s.at[0], lt_r.at[0], twin).start()

    r_slot = lax.rem(z, 2) * 2 + c

    @pl.when(c == z // 2)
    def _():
        pltpu.make_async_copy(r_out, r_in.at[r_slot], r_r.at[r_slot]).start()

    @pl.when(c != z // 2)
    def _():
        remote(r_out, r_in.at[r_slot], r_s.at[0], r_r.at[r_slot], twin).start()

    for n, d in enumerate((1, -1)):
        remote(
            r_out, r_in.at[r_slot], r_s.at[1 + n], r_r.at[r_slot], device(x, y, turn(z, d), z // 2)
        ).start()

    order = [0, 1, 3, 2]

    def psi_strip(group, first, last, part):
        return psi_in.at[group, first:last, pl.ds(pl.multiple_of(part * 32, 32), 32)]

    def psi_second(k):
        group = turn(y, -order[k])
        for slot in range(4):
            arrived(psi_quarter(group, slot, x), psi1_r.at[group * 4 + slot])
        part = psi_strip(group, 0, 4, x)
        for n, d in enumerate((1, -1)):
            remote(
                part, part, psi2_s.at[2 * k + n], psi2_r.at[4 * n + group],
                device(turn(x, d), y, z, c),
            ).start()

    def psi_further(k):
        d = k + k // 2 - 2 * (k // 3)
        group = turn(y, -d)
        for n, d in enumerate((1, -1)):
            arrived(psi_strip(group, 0, 4, turn(x, -d)), psi2_r.at[4 * n + group])
            part = psi_strip(group, 2 * n, 2 * n + 2, turn(x, -d))
            remote(
                part, part, psi2_s.at[8 + 2 * k + n], psi2_r.at[8 + 4 * n + group],
                device(turn(x, d), y, z, c),
            ).start()

    def left_further():
        for n, d in enumerate((1, -1)):
            came = turn(y, -d) * 2 + c
            arrived(l_in.at[came], l_r.at[2 - d])
            remote(l_in.at[came], l_in.at[came], lt_s.at[2 - d], lt_r.at[2 - d], twin).start()
            part = l_in.at[came, :, 32 * n : 32 * n + 32]
            remote(
                part, part, l_s.at[2 + n], l_r.at[4 + n], device(x, turn(y, d), z, c)
            ).start()

    near = turn(z, (1 - 2 * lax.rem(z, 2)) * (1 - 2 * as_int(c != z // 2)))
    onward = turn(z, z - near)
    near_pair = lax.rem(near, 2) * 2
    half = as_int(onward != turn(z, 1))

    def right_part(first, which):
        return r_in.at[
            pl.ds(first, 2), :, pl.ds(pl.multiple_of(which * 96, 32), 96)
        ]

    def right_further():
        for n in range(2):
            arrived(r_in.at[near_pair + n], r_r.at[near_pair + n])
        part = right_part(near_pair, half)
        remote(part, part, r_s.at[3], rf_r.at[half], device(x, y, onward, c)).start()

    psi_second(1)
    psi_second(2)
    psi_further(1)
    psi_second(3)
    left_further()
    right_further()

    gram_at = {}
    row = 5
    for k in range(4):
        for m in range(k, 4):
            gram_at[k, m] = row
            row += 1

    def gram(i, held):
        at = pl.ds(pl.multiple_of(i * 64, 64), 64)
        vectors = [sub[k, at, :].astype(jnp.float32) for k in range(4)]
        new = []
        for k in range(4):
            for m in range(k, 4):
                new.append(
                    held[len(new)]
                    + jnp.sum((vectors[k] * vectors[m]).reshape(8, 8, 128), axis=0)
                )
        return tuple(new)

    held = lax.fori_loop(
        0, 16, gram, tuple(jnp.zeros((8, 128), jnp.float32) for _ in range(10))
    )
    for k in range(10):
        mine[5 + k : 6 + k, :] = jnp.sum(held[k], axis=0, keepdims=True)

    def left_shard(group, core):
        for h in range(2):
            p = place_in_sector(lsec, group * 16 + z * 4 + core * 2 + h)
            weights = [
                (jnp.zeros((1, 256), jnp.int32) + as_int(p == at)).astype(jnp.bfloat16)
                for at in range(SEC_MOST)
            ]
            bands = l_in[group * 2 + core, :, :, h * PACKED : (h + 1) * PACKED].reshape(DEEP, PACKED)
            first = 2 + core * 2 + h
            rows = pl.ds(pl.multiple_of(group * 256 + core * 128 + h * TILE, TILE), TILE)
            for n in range(2):
                lanes = slice(n * 256, (n + 1) * 256)
                tiles = {
                    t: psi_in[group, t // 2, (t % 2) * TILE : (t % 2 + 1) * TILE, lanes]
                    for t in range(first - 2, first + 3)
                }
                source = jnp.concatenate(
                    [
                        tiles[first + m] * weights[0]
                        + tiles[first + m - 1] * weights[1]
                        + tiles[first + m - 2] * weights[2]
                        for m in range(SEC_MOST)
                    ],
                    axis=0,
                )
                made = jnp.dot(bands, source, preferred_element_type=jnp.float32).astype(
                    jnp.bfloat16
                )
                for w in range(TERMS):
                    mid[w, rows, lanes] = made[w * TILE : (w + 1) * TILE]

    def left_step(k, carry):
        d = k + k // 2 - 2 * (k // 3)
        group = turn(y, -d)
        own = l_in.at[group * 2 + c]

        @pl.when(k < 2)
        def _():
            psi_further(k + 2)

        @pl.when(k == 3)
        def _():
            for n in range(2):
                arrived(l_in.at[group * 2 + c, :, 32 * n : 32 * n + 32], l_r.at[4 + n])
            remote(own, own, lt_s.at[d], lt_r.at[d], twin).start()

        @pl.when(k == 0)
        def _():
            for slot in range(4):
                arrived(psi_in.at[y, slot], psi1_r.at[y * 4 + slot])

        @pl.when(k > 0)
        def _():
            for n in range(2):
                arrived(
                    psi_strip(group, 2 * n, 2 * n + 2, turn(x, 2)), psi2_r.at[8 + 4 * n + group]
                )

        arrived(l_in.at[group * 2 + 1 - c], lt_r.at[d])
        left_shard(group, 0)
        left_shard(group, 1)
        return carry

    lax.fori_loop(0, 4, left_step, 0)

    for d in range(4):
        zt = turn(z, d)
        part = sub.at[:, pl.ds(pl.multiple_of(zt * 256, 256), 256)]
        if d == 0:
            @pl.when(c == z // 2)
            def _(part=part):
                pltpu.make_async_copy(part, sub_in.at[r_slot], sub_r.at[r_slot]).start()

            @pl.when(c != z // 2)
            def _(part=part):
                remote(part, sub_in.at[r_slot], sub_s.at[0], sub_r.at[r_slot], twin).start()
        else:
            remote(
                part, sub_in.at[r_slot], sub_s.at[d], sub_r.at[r_slot], device(x, y, zt, z // 2)
            ).start()

    @pl.when(c == z // 2)
    def _():
        first = lax.rem(z, 2) * 2
        for n in range(2):
            arrived(r_in.at[first + n], r_r.at[first + n])

    @pl.when(c != z // 2)
    def _():
        for n in range(2):
            arrived(right_part(lax.rem(z, 2) * 2, n), rf_r.at[n])

    for b in range(4):
        place = [place_in_sector(rsec, y * 16 + c * 8 + b * 2 + h) for h in range(2)]
        weights = {}
        for i in range(6):
            for m in range(SEC_MOST):
                weights[i, m] = lanes_of(
                    as_int(place[0] == m - i + 2), as_int(place[1] == m - i + 3)
                ).astype(jnp.bfloat16)
        for w in range(TERMS):
            parts = [r_in[b, w, m * TILE : (m + 1) * TILE, :] for m in range(SEC_MOST)]
            for i in range(6):
                total = None
                for m in range(SEC_MOST):
                    if 0 <= m - i + 3 <= 3:
                        term = parts[m] * weights[i, m]
                        total = term if total is None else total + term
                r_wide[b, i * TILE : (i + 1) * TILE, w * 128 : (w + 1) * 128] = total

    def right_block(g, b):
        rows = pl.ds(pl.multiple_of(g * 256, 256), 256)
        source = jnp.concatenate(
            [mid[w, rows, b * 128 : (b + 1) * 128] for w in range(TERMS)], axis=1
        )
        out[rows, b * 128 : b * 128 + 384] += lax.dot_general(
            source, r_wide[b], (((1,), (1,)), ((), ())), preferred_element_type=jnp.float32
        )

    left_next = device(x, turn(y, -1 * as_int(c == 0)), z, 1 - c)
    right_next = device(x, turn(y, as_int(c == 1)), z, 1 - c)

    def right_step(i, carry):
        g = turn(x, i + 1)
        rows = pl.ds(pl.multiple_of(g * 256, 256), 256)
        right_block(g, 0)
        right_block(g, 3)
        halo_out[0, rows] = out[rows, 0:128].astype(jnp.bfloat16)
        halo_out[1, rows] = out[rows, 640:768].astype(jnp.bfloat16)
        remote(
            halo_out.at[0, rows], halo_in.at[1, rows], halo_s.at[i], halo_r.at[4 + i], left_next
        ).start()
        remote(
            halo_out.at[1, rows], halo_in.at[0, rows], halo_s.at[4 + i], halo_r.at[i], right_next
        ).start()
        right_block(g, 1)
        right_block(g, 2)

        @pl.when(i < 3)
        def _():
            rs_out[0, i] = out[rows, 256:512].astype(jnp.bfloat16)
            remote(
                rs_out.at[0, i], rs_in.at[0, i], rs_s.at[i], rs_r.at[i], device(g, y, z, c)
            ).start()

        return carry

    lax.fori_loop(0, 4, right_step, 0)

    def edge_columns(i, g):
        rows = pl.ds(pl.multiple_of(g * 256, 256), 256)
        for side in range(2):
            arrived(halo_in.at[side, rows], halo_r.at[4 * side + i])
        return (
            out[rows, 128:256] + halo_in[0, rows].astype(jnp.float32),
            out[rows, 512:640] + halo_in[1, rows].astype(jnp.float32),
        )

    def edge_step(i, carry):
        g = turn(x, i + 1)
        for n, total in enumerate(edge_columns(i, g)):
            rs_out[1, i, :, n * 128 : (n + 1) * 128] = total.astype(jnp.bfloat16)
        remote(
            rs_out.at[1, i], rs_in.at[1, i], rs_s.at[3 + i], rs_r.at[3 + i], device(g, y, z, c)
        ).start()
        return carry

    lax.fori_loop(0, 3, edge_step, 0)

    own_group = pl.ds(pl.multiple_of(x * 256, 256), 256)
    place_rows = pl.ds(pl.multiple_of(z * 256, 256), 256)
    held = [jnp.zeros((8, 128), jnp.float32) for _ in range(5)]
    for turn_of in range(2):
        if turn_of == 0:
            kept = (out[own_group, 256:384], out[own_group, 384:512])
        else:
            kept = edge_columns(3, x)
        for i in range(3):
            arrived(rs_in.at[turn_of, i], rs_r.at[3 * turn_of + i])
        for n in range(2):
            b = (1 + n) if turn_of == 0 else 3 * n
            total = kept[n]
            for i in range(3):
                total = total + rs_in[turn_of, i, :, n * 128 : (n + 1) * 128].astype(jnp.float32)
            zt, ct = 2 * c + b // 2, b % 2
            here = (z == zt) & (c == ct)

            @pl.when(here)
            def _(total=total):
                app[place_rows] = total

            @pl.when(jnp.logical_not(here))
            def _(total=total, b=b, zt=zt, ct=ct):
                deal[b] = total
                remote(
                    deal.at[b], app.at[place_rows], deal_s.at[b], deal_r.at[z],
                    device(x, y, zt, ct),
                ).start()

            arrived(sub_in.at[b], sub_r.at[b])
            products = [total * total] + [
                sub_in[b, k].astype(jnp.float32) * total for k in range(4)
            ]
            for k in range(5):
                held[k] = held[k] + jnp.sum(products[k].reshape(32, 8, 128), axis=0)
    for k in range(5):
        mine[k : k + 1, :] = jnp.sum(held[k], axis=0, keepdims=True)
    both = mine[...]
    both = both + pltpu.roll(both, TILE, 1)
    low_lanes = lax.broadcasted_iota(jnp.int32, (8, 128), 1) < TILE
    folded[...] = jnp.where(low_lanes, both[:8], both[8:])

    copies = []
    for d in range(1, 16):
        other = lax.rem(x * 4 + y + d, 16)
        copy = remote(
            folded, first_in.at[d - 1], send_c.at[d - 1], recv_c.at[d - 1],
            (other // 4, lax.rem(other, 4) * 8 + q),
        )
        copy.start()
        copies.append(copy)
    for copy in copies:
        copy.wait()
    added = folded[...]
    for d in range(15):
        added = added + first_in[d]
    second_out[...] = added
    copies = []
    for d in range(1, 8):
        copy = remote(
            second_out, second_in.at[d - 1], send_d.at[d - 1], recv_d.at[d - 1],
            (x, y * 8 + lax.rem(q + d, 8)),
        )
        copy.start()
        copies.append(copy)
    for copy in copies:
        copy.wait()
    for d in range(7):
        added = added + second_in[d]
    sums_all = jnp.concatenate(
        [
            jnp.sum(jnp.where(low_lanes, added, 0.0), axis=1, keepdims=True),
            jnp.sum(jnp.where(low_lanes, 0.0, added), axis=1, keepdims=True),
        ],
        axis=0,
    )

    def one(i):
        return sums_all[i : i + 1, :] * (1.0 / float(D_LEFT * D_RIGHT))

    coefficient = [one(1 + k) / (one(gram_at[k, k]) + epsilon) for k in range(4)]
    energy = one(0)
    for k in range(4):
        energy = energy - 2.0 * coefficient[k] * one(1 + k)
        for m in range(k, 4):
            twice = 1.0 if m == k else 2.0
            energy = energy + twice * coefficient[k] * coefficient[m] * one(gram_at[k, m])
    scale = lax.rsqrt(jnp.maximum(energy, 0.0) + epsilon)

    def write(i, carry):
        rows = pl.ds(pl.multiple_of(i * 128, 128), 128)
        block = app[rows]
        residual = block
        for k in range(4):
            residual = residual - coefficient[k] * sub[k, rows, :].astype(jnp.float32)
        applied_ref[rows, :] = block
        vector_ref[rows, :] = residual * scale
        return carry

    for i in range(4):
        @pl.when(jnp.logical_not((z == i) & (c == z // 2)))
        def _(i=i):
            arrived(app.at[i * 256 : (i + 1) * 256], deal_r.at[i])

    lax.fori_loop(0, 8, write, 0)

    for n in range(2):
        @pl.when(c != n)
        def _(n=n):
            left(psi_whole(y, n), psi1_s.at[n])

        left(psi_whole(y, n), psi1_s.at[8 + n])
    for n in range(2, 8):
        left(psi_part(y, 0), psi1_s.at[n])
        left(psi_part(y, 0), psi1_s.at[8 + n])

    @pl.when(c != z // 2)
    def _():
        left(r_out, r_s.at[0])
        left(sub.at[:, 0:256], sub_s.at[0])

    for d in range(1, 4):
        left(sub.at[:, 0:256], sub_s.at[d])
        left(rs_out.at[0, d - 1], rs_s.at[d - 1])
        left(rs_out.at[1, d - 1], rs_s.at[2 + d])
    for n in range(2, 8):
        left(psi_strip(0, 0, 4, x), psi2_s.at[n])
        left(psi_strip(0, 0, 2, x), psi2_s.at[8 + n])
    for n in range(2):
        left(l_mine, l_s.at[n])
        left(l_in.at[0, :, 0:32], l_s.at[2 + n])
        left(r_out, r_s.at[1 + n])
    left(right_part(near_pair, half), r_s.at[3])
    for g in range(4):
        left(l_mine, lt_s.at[g])
        left(halo_out.at[0, 0:256], halo_s.at[g])
        left(halo_out.at[1, 0:256], halo_s.at[4 + g])
        zt, ct = 2 * c + g // 2, g % 2

        @pl.when(jnp.logical_not((z == zt) & (c == ct)))
        def _(g=g):
            left(deal.at[g], deal_s.at[g])


def per_device(
    wavefunction, subspace, left_band, right_band, left_sector, right_sector, term_sectors
):
    shape = jax.ShapeDtypeStruct((1024, 128), jnp.float32)
    dma = pltpu.SemaphoreType.DMA
    bf16, f32 = jnp.bfloat16, jnp.float32
    vmem = pl.BlockSpec(memory_space=pltpu.VMEM)
    smem = pl.BlockSpec(memory_space=pltpu.SMEM)
    return pl.pallas_call(
        kernel,
        out_shape=(shape, shape),
        in_specs=[smem, smem, vmem, pl.BlockSpec(memory_space=pl.ANY), vmem, vmem, vmem],
        out_specs=(vmem, vmem),
        scratch_shapes=[
            pltpu.VMEM((8, TERMS, TILE, 2 * PACKED), bf16),
            pltpu.VMEM((TERMS, PACKED, 128), bf16),
            pltpu.VMEM((4, TERMS, PACKED, 128), bf16),
            pltpu.VMEM((4, 4, 128, 512), bf16),
            pltpu.VMEM((4, 384, TERMS * 128), bf16),
            pltpu.VMEM((TERMS, 1024, 512), bf16),
            pltpu.VMEM((1024, 768), f32),
            pltpu.VMEM((2, 1024, 128), bf16),
            pltpu.VMEM((2, 1024, 128), bf16),
            pltpu.VMEM((2, 3, 256, 256), bf16),
            pltpu.VMEM((2, 3, 256, 256), bf16),
            pltpu.VMEM((4, 4, 256, 128), bf16),
            pltpu.VMEM((4, 256, 128), f32),
            pltpu.VMEM((1024, 128), f32),
            pltpu.VMEM((16, 128), f32),
            pltpu.VMEM((8, 128), f32),
            pltpu.VMEM((15, 8, 128), f32),
            pltpu.VMEM((8, 128), f32),
            pltpu.VMEM((7, 8, 128), f32),
            dma((16,)), dma((16,)), dma((16,)), dma((16,)),
            dma((4,)), dma((4,)), dma((2,)), dma((4,)), dma((6,)), dma((4,)), dma((4,)),
            dma((8,)), dma((8,)), dma((6,)), dma((6,)), dma((4,)), dma((4,)), dma((4,)), dma((4,)),
            dma((15,)), dma((15,)), dma((7,)), dma((7,)),
        ],
        compiler_params=pltpu.CompilerParams(
            collective_id=0, has_side_effects=True, vmem_limit_bytes=56 * 1024 * 1024
        ),
        name="two_site_step",
    )(
        left_sector, right_sector, term_sectors, wavefunction, subspace,
        jnp.swapaxes(left_band, 1, 2), jnp.swapaxes(right_band, 1, 2),
    )


def solution(mesh):
    return jax.shard_map(
        per_device,
        mesh=mesh,
        in_specs=(
            P("bond", None),
            P(None, "mpo", "bond"),
            P("mpo", "bond", None),
            P("mpo", "bond", None),
            P(),
            P(),
            P("mpo", None),
        ),
        out_specs=(P("mpo", "bond"), P("mpo", "bond")),
        check_vma=False,
    )
```

```python
import functools

import jax
import jax.numpy as jnp
from jax import lax
from jax.experimental import pallas as pl
from jax.experimental.pallas import tpu as pltpu
from jax.sharding import PartitionSpec as P

D_LEFT = 4096
D_RIGHT = 4096
TILE = 64
SEC_MOST = 3
PACKED = SEC_MOST * TILE
NT = 64
TERMS = 9
DEEP = TERMS * TILE
MESH = pl.DeviceIdType.MESH

epsilon = 1e-06


def as_int(flag):
    return flag.astype(jnp.int32)


def place_in_sector(sector, tile):
    here = sector[tile]
    one = as_int((tile >= 1) & (sector[jnp.maximum(tile - 1, 0)] == here))
    two = as_int((tile >= 2) & (sector[jnp.maximum(tile - 2, 0)] == here))
    return one + two


def sector_size(sector, tile):
    here = sector[tile]
    one = as_int((tile <= NT - 2) & (sector[jnp.minimum(tile + 1, NT - 1)] == here))
    two = as_int((tile <= NT - 3) & (sector[jnp.minimum(tile + 2, NT - 1)] == here))
    return 1 + place_in_sector(sector, tile) + one + two


def lanes_of(low, high):
    half = lax.broadcasted_iota(jnp.int32, (1, 128), 1) // TILE
    return low * (1 - half) + high * half


def pack_masks(sector, first_tile):
    row = lax.broadcasted_iota(jnp.int32, (PACKED, 128), 0)
    place = [place_in_sector(sector, first_tile + h) for h in range(2)]
    size = [sector_size(sector, first_tile + h) * TILE for h in range(2)]
    return [
        jnp.clip(
            lanes_of(size[0] * as_int(place[0] == at), size[1] * as_int(place[1] == at)) - row, 0, 1
        ).astype(jnp.bfloat16)
        for at in range(SEC_MOST)
    ]


def packed_term(band, w, masks):
    total = band[w, 2 * TILE : 2 * TILE + PACKED, :] * masks[0]
    total = total + band[w, TILE : TILE + PACKED, :] * masks[1]
    return total + band[w, :PACKED, :] * masks[2]


def kernel(
    lsec, rsec, terms, psi, sub, lband, rband,
    app, stats_ref,
    l_in, r_out, r_in, psi_in, r_wide, mid, out, halo_out, halo_in, rs_out, rs_in, sub_in, deal,
    mine, folded, first_in, second_out, second_in,
    psi1_s, psi1_r, psi2_s, psi2_r, r_s, r_r, rf_r, l_s, l_r, lt_s, lt_r,
    halo_s, halo_r, rs_s, rs_r, sub_s, sub_r, deal_s, deal_r, send_c, recv_c, send_d, recv_d,
):
    x = lax.axis_index("mpo")
    bond = lax.axis_index("bond")
    y = bond // 8
    q = lax.rem(bond, 8)
    z = q // 2
    c = lax.rem(q, 2)

    def device(dx, dy, dz, dc):
        return (dx, dy * 8 + dz * 2 + dc)

    def turn(value, step):
        return lax.rem(value + step + 4, 4)

    def remote(src, dst, send, recv, target):
        return pltpu.make_async_remote_copy(
            src_ref=src, dst_ref=dst, send_sem=send, recv_sem=recv,
            device_id=target, device_id_type=MESH,
        )

    twin = device(x, y, z, 1 - c)

    def arrived(dst, recv):
        remote(dst, dst, l_s.at[0], recv, twin).wait_recv()

    def left(src, send):
        remote(src, src, send, l_r.at[0], twin).wait_send()

    def signal(target):
        pl.semaphore_signal(barrier, inc=1, device_id=target, device_id_type=MESH)

    barrier = pltpu.get_barrier_semaphore()
    for d in range(1, 8):
        signal((x, y * 8 + lax.rem(q + d, 8)))
    for d in range(1, 16):
        other = lax.rem(x * 4 + y + d, 16)
        signal((other // 4, lax.rem(other, 4) * 8 + q))
    for d in range(1, 4):
        signal(device(x, turn(y, d), z, 1 - c))
        signal(device(x, turn(y, d), turn(z, -1), 1))
        signal(device(x, turn(y, d), turn(z, 1), 0))
    masks = pack_masks(lsec, bond * 2)
    number = lax.broadcasted_iota(jnp.int32, terms.shape, 1)
    active = []
    for h in range(2):
        same = 1 - jnp.clip(jnp.abs(number - lsec[bond * 2 + h]), 0, 1)
        active.append(jnp.sum(terms[...] * same, axis=1, keepdims=True))
    l_mine = l_in.at[y * 2 + c]
    for w in range(TERMS):
        switch = lanes_of(active[0][w : w + 1], active[1][w : w + 1]).astype(jnp.bfloat16)
        rows = (packed_term(lband, w, masks) * switch).T
        l_in[y * 2 + c, w] = jnp.concatenate([rows[:TILE], rows[TILE:]], axis=1)
    masks = pack_masks(rsec, bond * 2)
    for w in range(TERMS):
        r_out[w] = packed_term(rband, w, masks)
    mine[...] = jnp.zeros_like(mine)
    out[...] = jnp.zeros_like(out)
    pl.semaphore_wait(barrier, 31)

    above = as_int((z == 3) & (c == 1))
    below = as_int((z == 0) & (c == 0))
    halo_y = turn(y, above - below)
    halo_z = turn(z, 2 * c - 1)
    halo_slot = 3 * (1 - c)
    own_rows = pl.ds(pl.multiple_of(x * 32, 32), 32)

    def psi_columns(dy, k):
        return pl.ds(pl.multiple_of(dy * 1024 + k * 512, 512), 512)

    def psi_part(dy, k):
        return psi.at[own_rows, psi_columns(dy, k)]

    def psi_whole(dy, k):
        return psi.at[:, psi_columns(dy, k)]

    def psi_quarter(group, slot, part):
        return psi_in.at[group, slot, pl.ds(pl.multiple_of(part * 32, 32), 32)]

    for k in range(2):
        @pl.when(c == k)
        def _(k=k):
            pltpu.make_async_copy(
                psi_whole(y, k), psi_in.at[y, 1 + c], psi1_r.at[y * 4 + 1 + c]
            ).start()

        @pl.when(c != k)
        def _(k=k):
            remote(
                psi_whole(y, k), psi_in.at[y, 1 + c], psi1_s.at[k], psi1_r.at[y * 4 + 1 + c], twin
            ).start()

    for d in (1, 3, 2, 0):
        dy = turn(y, d)
        hy = turn(halo_y, d)
        for k in range(2):
            n = 2 * d + k
            if d > 0:
                remote(
                    psi_part(dy, k), psi_quarter(y, 1 + c, x), psi1_s.at[n],
                    psi1_r.at[y * 4 + 1 + c], device(x, dy, z, k),
                ).start()
                source, target = psi_part(hy, k), psi_quarter(halo_y, halo_slot, x)
            else:
                source, target = psi_whole(hy, k), psi_in.at[halo_y, halo_slot]
            remote(
                source, target, psi1_s.at[8 + n], psi1_r.at[halo_y * 4 + halo_slot],
                device(x, hy, halo_z, k),
            ).start()

    remote(l_mine, l_mine, l_s.at[0], l_r.at[1], device(x, turn(y, 1), z, c)).start()
    remote(l_mine, l_mine, l_s.at[1], l_r.at[3], device(x, turn(y, -1), z, c)).start()
    remote(l_mine, l_mine, lt_s.at[0], lt_r.at[0], twin).start()

    r_slot = lax.rem(z, 2) * 2 + c

    @pl.when(c == z // 2)
    def _():
        pltpu.make_async_copy(r_out, r_in.at[r_slot], r_r.at[r_slot]).start()

    @pl.when(c != z // 2)
    def _():
        remote(r_out, r_in.at[r_slot], r_s.at[0], r_r.at[r_slot], twin).start()

    for n, d in enumerate((1, -1)):
        remote(
            r_out, r_in.at[r_slot], r_s.at[1 + n], r_r.at[r_slot], device(x, y, turn(z, d), z // 2)
        ).start()

    order = [0, 1, 3, 2]

    def psi_strip(group, first, last, part):
        return psi_in.at[group, first:last, pl.ds(pl.multiple_of(part * 32, 32), 32)]

    def psi_second(k):
        group = turn(y, -order[k])
        for slot in range(4):
            arrived(psi_quarter(group, slot, x), psi1_r.at[group * 4 + slot])
        part = psi_strip(group, 0, 4, x)
        for n, d in enumerate((1, -1)):
            remote(
                part, part, psi2_s.at[2 * k + n], psi2_r.at[4 * n + group],
                device(turn(x, d), y, z, c),
            ).start()

    def psi_further(k):
        d = k + k // 2 - 2 * (k // 3)
        group = turn(y, -d)
        for n, d in enumerate((1, -1)):
            arrived(psi_strip(group, 0, 4, turn(x, -d)), psi2_r.at[4 * n + group])
            part = psi_strip(group, 2 * n, 2 * n + 2, turn(x, -d))
            remote(
                part, part, psi2_s.at[8 + 2 * k + n], psi2_r.at[8 + 4 * n + group],
                device(turn(x, d), y, z, c),
            ).start()

    def left_further():
        for n, d in enumerate((1, -1)):
            came = turn(y, -d) * 2 + c
            arrived(l_in.at[came], l_r.at[2 - d])
            remote(l_in.at[came], l_in.at[came], lt_s.at[2 - d], lt_r.at[2 - d], twin).start()
            part = l_in.at[came, :, 32 * n : 32 * n + 32]
            remote(
                part, part, l_s.at[2 + n], l_r.at[4 + n], device(x, turn(y, d), z, c)
            ).start()

    near = turn(z, (1 - 2 * lax.rem(z, 2)) * (1 - 2 * as_int(c != z // 2)))
    onward = turn(z, z - near)
    near_pair = lax.rem(near, 2) * 2
    half = as_int(onward != turn(z, 1))

    def right_part(first, which):
        return r_in.at[
            pl.ds(first, 2), :, pl.ds(pl.multiple_of(which * 96, 32), 96)
        ]

    def right_further():
        for n in range(2):
            arrived(r_in.at[near_pair + n], r_r.at[near_pair + n])
        part = right_part(near_pair, half)
        remote(part, part, r_s.at[3], rf_r.at[half], device(x, y, onward, c)).start()

    psi_second(1)
    psi_second(2)
    psi_second(3)
    psi_further(1)
    right_further()
    left_further()

    gram_at = {}
    row = 5
    for k in range(4):
        for m in range(k, 4):
            gram_at[k, m] = row
            row += 1

    def gram(i, held):
        at = pl.ds(pl.multiple_of(i * 64, 64), 64)
        vectors = [sub[k, at, :].astype(jnp.float32) for k in range(4)]
        new = []
        for k in range(4):
            for m in range(k, 4):
                new.append(
                    held[len(new)]
                    + jnp.sum((vectors[k] * vectors[m]).reshape(8, 8, 128), axis=0)
                )
        return tuple(new)

    held = lax.fori_loop(
        0, 16, gram, tuple(jnp.zeros((8, 128), jnp.float32) for _ in range(10))
    )
    for k in range(10):
        mine[5 + k : 6 + k, :] = jnp.sum(held[k], axis=0, keepdims=True)

    def left_shard(group, core):
        for h in range(2):
            p = place_in_sector(lsec, group * 16 + z * 4 + core * 2 + h)
            weights = [
                (jnp.zeros((1, 256), jnp.int32) + as_int(p == at)).astype(jnp.bfloat16)
                for at in range(SEC_MOST)
            ]
            bands = l_in[group * 2 + core, :, :, h * PACKED : (h + 1) * PACKED].reshape(DEEP, PACKED)
            first = 2 + core * 2 + h
            rows = pl.ds(pl.multiple_of(group * 256 + core * 128 + h * TILE, TILE), TILE)
            for n in range(2):
                lanes = slice(n * 256, (n + 1) * 256)
                tiles = {
                    t: psi_in[group, t // 2, (t % 2) * TILE : (t % 2 + 1) * TILE, lanes]
                    for t in range(first - 2, first + 3)
                }
                source = jnp.concatenate(
                    [
                        tiles[first + m] * weights[0]
                        + tiles[first + m - 1] * weights[1]
                        + tiles[first + m - 2] * weights[2]
                        for m in range(SEC_MOST)
                    ],
                    axis=0,
                )
                made = jnp.dot(bands, source, preferred_element_type=jnp.float32).astype(
                    jnp.bfloat16
                )
                for w in range(TERMS):
                    mid[w, rows, lanes] = made[w * TILE : (w + 1) * TILE]

    def left_step(k, carry):
        d = k + k // 2 - 2 * (k // 3)
        group = turn(y, -d)
        own = l_in.at[group * 2 + c]

        @pl.when(k < 2)
        def _():
            psi_further(k + 2)

        @pl.when(k == 3)
        def _():
            for n in range(2):
                arrived(l_in.at[group * 2 + c, :, 32 * n : 32 * n + 32], l_r.at[4 + n])
            remote(own, own, lt_s.at[d], lt_r.at[d], twin).start()

        @pl.when(k == 0)
        def _():
            for slot in range(4):
                arrived(psi_in.at[y, slot], psi1_r.at[y * 4 + slot])

        @pl.when(k > 0)
        def _():
            for n in range(2):
                arrived(
                    psi_strip(group, 2 * n, 2 * n + 2, turn(x, 2)), psi2_r.at[8 + 4 * n + group]
                )

        arrived(l_in.at[group * 2 + 1 - c], lt_r.at[d])
        left_shard(group, 0)
        left_shard(group, 1)
        return carry

    lax.fori_loop(0, 4, left_step, 0)

    for d in range(4):
        zt = turn(z, d)
        part = sub.at[:, pl.ds(pl.multiple_of(zt * 256, 256), 256)]
        if d == 0:
            @pl.when(c == z // 2)
            def _(part=part):
                pltpu.make_async_copy(part, sub_in.at[r_slot], sub_r.at[r_slot]).start()

            @pl.when(c != z // 2)
            def _(part=part):
                remote(part, sub_in.at[r_slot], sub_s.at[0], sub_r.at[r_slot], twin).start()
        else:
            remote(
                part, sub_in.at[r_slot], sub_s.at[d], sub_r.at[r_slot], device(x, y, zt, z // 2)
            ).start()

    @pl.when(c == z // 2)
    def _():
        first = lax.rem(z, 2) * 2
        for n in range(2):
            arrived(r_in.at[first + n], r_r.at[first + n])

    @pl.when(c != z // 2)
    def _():
        for n in range(2):
            arrived(right_part(lax.rem(z, 2) * 2, n), rf_r.at[n])

    for b in range(4):
        place = [place_in_sector(rsec, y * 16 + c * 8 + b * 2 + h) for h in range(2)]
        weights = {}
        for i in range(6):
            for m in range(SEC_MOST):
                weights[i, m] = lanes_of(
                    as_int(place[0] == m - i + 2), as_int(place[1] == m - i + 3)
                ).astype(jnp.bfloat16)
        for w in range(TERMS):
            parts = [r_in[b, w, m * TILE : (m + 1) * TILE, :] for m in range(SEC_MOST)]
            for i in range(6):
                total = None
                for m in range(SEC_MOST):
                    if 0 <= m - i + 3 <= 3:
                        term = parts[m] * weights[i, m]
                        total = term if total is None else total + term
                r_wide[b, i * TILE : (i + 1) * TILE, w * 128 : (w + 1) * 128] = total

    def right_block(g, b):
        rows = pl.ds(pl.multiple_of(g * 256, 256), 256)
        source = jnp.concatenate(
            [mid[w, rows, b * 128 : (b + 1) * 128] for w in range(TERMS)], axis=1
        )
        out[rows, b * 128 : b * 128 + 384] += lax.dot_general(
            source, r_wide[b], (((1,), (1,)), ((), ())), preferred_element_type=jnp.float32
        )

    left_next = device(x, turn(y, -1 * as_int(c == 0)), z, 1 - c)
    right_next = device(x, turn(y, as_int(c == 1)), z, 1 - c)

    def right_step(i, carry):
        g = turn(x, i + 1)
        rows = pl.ds(pl.multiple_of(g * 256, 256), 256)
        right_block(g, 0)
        right_block(g, 3)
        halo_out[0, rows] = out[rows, 0:128].astype(jnp.bfloat16)
        halo_out[1, rows] = out[rows, 640:768].astype(jnp.bfloat16)
        remote(
            halo_out.at[0, rows], halo_in.at[1, rows], halo_s.at[i], halo_r.at[4 + i], left_next
        ).start()
        remote(
            halo_out.at[1, rows], halo_in.at[0, rows], halo_s.at[4 + i], halo_r.at[i], right_next
        ).start()
        right_block(g, 1)
        right_block(g, 2)

        @pl.when(i < 3)
        def _():
            rs_out[0, i] = out[rows, 256:512].astype(jnp.bfloat16)
            remote(
                rs_out.at[0, i], rs_in.at[0, i], rs_s.at[i], rs_r.at[i], device(g, y, z, c)
            ).start()

        return carry

    lax.fori_loop(0, 4, right_step, 0)

    def edge_columns(i, g):
        rows = pl.ds(pl.multiple_of(g * 256, 256), 256)
        for side in range(2):
            arrived(halo_in.at[side, rows], halo_r.at[4 * side + i])
        return (
            out[rows, 128:256] + halo_in[0, rows].astype(jnp.float32),
            out[rows, 512:640] + halo_in[1, rows].astype(jnp.float32),
        )

    def edge_step(i, carry):
        g = turn(x, i + 1)
        for n, total in enumerate(edge_columns(i, g)):
            rs_out[1, i, :, n * 128 : (n + 1) * 128] = total.astype(jnp.bfloat16)
        remote(
            rs_out.at[1, i], rs_in.at[1, i], rs_s.at[3 + i], rs_r.at[3 + i], device(g, y, z, c)
        ).start()
        return carry

    lax.fori_loop(0, 3, edge_step, 0)

    own_group = pl.ds(pl.multiple_of(x * 256, 256), 256)
    place_rows = pl.ds(pl.multiple_of(z * 256, 256), 256)
    held = [jnp.zeros((8, 128), jnp.float32) for _ in range(5)]
    for turn_of in range(2):
        if turn_of == 0:
            kept = (out[own_group, 256:384], out[own_group, 384:512])
        else:
            kept = edge_columns(3, x)
        for i in range(3):
            arrived(rs_in.at[turn_of, i], rs_r.at[3 * turn_of + i])
        for n in range(2):
            b = (1 + n) if turn_of == 0 else 3 * n
            total = kept[n]
            for i in range(3):
                total = total + rs_in[turn_of, i, :, n * 128 : (n + 1) * 128].astype(jnp.float32)
            zt, ct = 2 * c + b // 2, b % 2
            here = (z == zt) & (c == ct)

            @pl.when(here)
            def _(total=total):
                app[place_rows] = total

            @pl.when(jnp.logical_not(here))
            def _(total=total, b=b, zt=zt, ct=ct):
                deal[b] = total
                remote(
                    deal.at[b], app.at[place_rows], deal_s.at[b], deal_r.at[z],
                    device(x, y, zt, ct),
                ).start()

            arrived(sub_in.at[b], sub_r.at[b])
            products = [total * total] + [
                sub_in[b, k].astype(jnp.float32) * total for k in range(4)
            ]
            for k in range(5):
                held[k] = held[k] + jnp.sum(products[k].reshape(32, 8, 128), axis=0)
    for k in range(5):
        mine[k : k + 1, :] = jnp.sum(held[k], axis=0, keepdims=True)
    both = mine[...]
    both = both + pltpu.roll(both, TILE, 1)
    low_lanes = lax.broadcasted_iota(jnp.int32, (8, 128), 1) < TILE
    folded[...] = jnp.where(low_lanes, both[:8], both[8:])

    copies = []
    for d in range(1, 16):
        other = lax.rem(x * 4 + y + d, 16)
        copy = remote(
            folded, first_in.at[d - 1], send_c.at[d - 1], recv_c.at[d - 1],
            (other // 4, lax.rem(other, 4) * 8 + q),
        )
        copy.start()
        copies.append(copy)
    for copy in copies:
        copy.wait()
    added = folded[...]
    for d in range(15):
        added = added + first_in[d]
    second_out[...] = added
    copies = []
    for d in range(1, 8):
        copy = remote(
            second_out, second_in.at[d - 1], send_d.at[d - 1], recv_d.at[d - 1],
            (x, y * 8 + lax.rem(q + d, 8)),
        )
        copy.start()
        copies.append(copy)
    for copy in copies:
        copy.wait()
    for d in range(7):
        added = added + second_in[d]
    sums_all = jnp.concatenate(
        [
            jnp.sum(jnp.where(low_lanes, added, 0.0), axis=1, keepdims=True),
            jnp.sum(jnp.where(low_lanes, 0.0, added), axis=1, keepdims=True),
        ],
        axis=0,
    )

    def one(i):
        return sums_all[i : i + 1, :] * (1.0 / float(D_LEFT * D_RIGHT))

    coefficient = [one(1 + k) / (one(gram_at[k, k]) + epsilon) for k in range(4)]
    energy = one(0)
    for k in range(4):
        energy = energy - 2.0 * coefficient[k] * one(1 + k)
        for m in range(k, 4):
            twice = 1.0 if m == k else 2.0
            energy = energy + twice * coefficient[k] * coefficient[m] * one(gram_at[k, m])
    scale = lax.rsqrt(jnp.maximum(energy, 0.0) + epsilon)

    for i in range(4):
        @pl.when(jnp.logical_not((z == i) & (c == z // 2)))
        def _(i=i):
            arrived(app.at[i * 256 : (i + 1) * 256], deal_r.at[i])

    for n, value in enumerate(coefficient + [scale]):
        stats_ref[n : n + 1, :] = jnp.zeros((1, 128), jnp.float32) + value
    stats_ref[5:8, :] = jnp.zeros((3, 128), jnp.float32)

    for n in range(2):
        @pl.when(c != n)
        def _(n=n):
            left(psi_whole(y, n), psi1_s.at[n])

        left(psi_whole(y, n), psi1_s.at[8 + n])
    for n in range(2, 8):
        left(psi_part(y, 0), psi1_s.at[n])
        left(psi_part(y, 0), psi1_s.at[8 + n])

    @pl.when(c != z // 2)
    def _():
        left(r_out, r_s.at[0])
        left(sub.at[:, 0:256], sub_s.at[0])

    for d in range(1, 4):
        left(sub.at[:, 0:256], sub_s.at[d])
        left(rs_out.at[0, d - 1], rs_s.at[d - 1])
        left(rs_out.at[1, d - 1], rs_s.at[2 + d])
    for n in range(2, 8):
        left(psi_strip(0, 0, 4, x), psi2_s.at[n])
        left(psi_strip(0, 0, 2, x), psi2_s.at[8 + n])
    for n in range(2):
        left(l_mine, l_s.at[n])
        left(l_in.at[0, :, 0:32], l_s.at[2 + n])
        left(r_out, r_s.at[1 + n])
    left(right_part(near_pair, half), r_s.at[3])
    for g in range(4):
        left(l_mine, lt_s.at[g])
        left(halo_out.at[0, 0:256], halo_s.at[g])
        left(halo_out.at[1, 0:256], halo_s.at[4 + g])
        zt, ct = 2 * c + g // 2, g % 2

        @pl.when(jnp.logical_not((z == zt) & (c == ct)))
        def _(g=g):
            left(deal.at[g], deal_s.at[g])


def write_kernel(stats_ref, app_ref, sub_ref, applied_ref, vector_ref):
    residual = app_ref[...]
    applied_ref[...] = residual
    for k in range(4):
        residual = residual - stats_ref[k : k + 1, :] * sub_ref[k].astype(jnp.float32)
    vector_ref[...] = residual * stats_ref[4:5, :]


def per_device(
    wavefunction, subspace, left_band, right_band, left_sector, right_sector, term_sectors
):
    shape = jax.ShapeDtypeStruct((1024, 128), jnp.float32)
    dma = pltpu.SemaphoreType.DMA
    bf16, f32 = jnp.bfloat16, jnp.float32
    vmem = pl.BlockSpec(memory_space=pltpu.VMEM)
    smem = pl.BlockSpec(memory_space=pltpu.SMEM)
    app, stats = pl.pallas_call(
        kernel,
        out_shape=(shape, jax.ShapeDtypeStruct((8, 128), f32)),
        in_specs=[smem, smem, vmem, pl.BlockSpec(memory_space=pl.ANY), vmem, vmem, vmem],
        out_specs=(vmem, vmem),
        scratch_shapes=[
            pltpu.VMEM((8, TERMS, TILE, 2 * PACKED), bf16),
            pltpu.VMEM((TERMS, PACKED, 128), bf16),
            pltpu.VMEM((4, TERMS, PACKED, 128), bf16),
            pltpu.VMEM((4, 4, 128, 512), bf16),
            pltpu.VMEM((4, 384, TERMS * 128), bf16),
            pltpu.VMEM((TERMS, 1024, 512), bf16),
            pltpu.VMEM((1024, 768), f32),
            pltpu.VMEM((2, 1024, 128), bf16),
            pltpu.VMEM((2, 1024, 128), bf16),
            pltpu.VMEM((2, 3, 256, 256), bf16),
            pltpu.VMEM((2, 3, 256, 256), bf16),
            pltpu.VMEM((4, 4, 256, 128), bf16),
            pltpu.VMEM((4, 256, 128), f32),
            pltpu.VMEM((16, 128), f32),
            pltpu.VMEM((8, 128), f32),
            pltpu.VMEM((15, 8, 128), f32),
            pltpu.VMEM((8, 128), f32),
            pltpu.VMEM((7, 8, 128), f32),
            dma((16,)), dma((16,)), dma((16,)), dma((16,)),
            dma((4,)), dma((4,)), dma((2,)), dma((4,)), dma((6,)), dma((4,)), dma((4,)),
            dma((8,)), dma((8,)), dma((6,)), dma((6,)), dma((4,)), dma((4,)), dma((4,)), dma((4,)),
            dma((15,)), dma((15,)), dma((7,)), dma((7,)),
        ],
        compiler_params=pltpu.CompilerParams(
            collective_id=0, has_side_effects=True, vmem_limit_bytes=56 * 1024 * 1024
        ),
        name="two_site_step",
    )(
        left_sector, right_sector, term_sectors, wavefunction, subspace,
        jnp.swapaxes(left_band, 1, 2), jnp.swapaxes(right_band, 1, 2),
    )
    each = 512
    block = pl.BlockSpec((each, 128), lambda i: (i, 0))
    return pl.pallas_call(
        write_kernel,
        grid=(1024 // each,),
        out_shape=(shape, shape),
        in_specs=[
            pl.BlockSpec((8, 128), lambda i: (0, 0)),
            block,
            pl.BlockSpec((4, each, 128), lambda i: (0, i, 0)),
        ],
        out_specs=(block, block),
        name="write_results",
    )(stats, app, subspace)


def solution(mesh):
    return jax.shard_map(
        per_device,
        mesh=mesh,
        in_specs=(
            P("bond", None),
            P(None, "mpo", "bond"),
            P("mpo", "bond", None),
            P("mpo", "bond", None),
            P(),
            P(),
            P("mpo", None),
        ),
        out_specs=(P("mpo", "bond"), P("mpo", "bond")),
        check_vma=False,
    )
```

```python
import functools

import jax
import jax.numpy as jnp
from jax import lax
from jax.experimental import pallas as pl
from jax.experimental.pallas import tpu as pltpu
from jax.sharding import PartitionSpec as P

D_LEFT = 4096
D_RIGHT = 4096
TILE = 64
SEC_MOST = 3
PACKED = SEC_MOST * TILE
NT = 64
TERMS = 9
DEEP = TERMS * TILE
MESH = pl.DeviceIdType.MESH

epsilon = 1e-06


def as_int(flag):
    return flag.astype(jnp.int32)


def place_in_sector(sector, tile):
    here = sector[tile]
    one = as_int((tile >= 1) & (sector[jnp.maximum(tile - 1, 0)] == here))
    two = as_int((tile >= 2) & (sector[jnp.maximum(tile - 2, 0)] == here))
    return one + two


def sector_size(sector, tile):
    here = sector[tile]
    one = as_int((tile <= NT - 2) & (sector[jnp.minimum(tile + 1, NT - 1)] == here))
    two = as_int((tile <= NT - 3) & (sector[jnp.minimum(tile + 2, NT - 1)] == here))
    return 1 + place_in_sector(sector, tile) + one + two


def lanes_of(low, high):
    half = lax.broadcasted_iota(jnp.int32, (1, 128), 1) // TILE
    return low * (1 - half) + high * half


def pack_masks(sector, first_tile):
    row = lax.broadcasted_iota(jnp.int32, (PACKED, 128), 0)
    place = [place_in_sector(sector, first_tile + h) for h in range(2)]
    size = [sector_size(sector, first_tile + h) * TILE for h in range(2)]
    return [
        jnp.clip(
            lanes_of(size[0] * as_int(place[0] == at), size[1] * as_int(place[1] == at)) - row, 0, 1
        ).astype(jnp.bfloat16)
        for at in range(SEC_MOST)
    ]


def packed_term(band, w, masks):
    total = band[w, 2 * TILE : 2 * TILE + PACKED, :] * masks[0]
    total = total + band[w, TILE : TILE + PACKED, :] * masks[1]
    return total + band[w, :PACKED, :] * masks[2]


def kernel(
    lsec, rsec, terms, psi, sub, lband, rband,
    app, stats_ref,
    l_in, r_out, r_in, psi_in, r_wide, mid, out, halo_out, halo_in, rs_out, rs_in, sub_in, deal,
    mine, folded, first_in, second_out, second_in,
    psi1_s, psi1_r, psi2_s, psi2_r, r_s, r_r, rf_r, l_s, l_r, lt_s, lt_r,
    halo_s, halo_r, rs_s, rs_r, sub_s, sub_r, deal_s, deal_r, send_c, recv_c, send_d, recv_d,
):
    x = lax.axis_index("mpo")
    bond = lax.axis_index("bond")
    y = bond // 8
    q = lax.rem(bond, 8)
    z = q // 2
    c = lax.rem(q, 2)

    def device(dx, dy, dz, dc):
        return (dx, dy * 8 + dz * 2 + dc)

    def turn(value, step):
        return lax.rem(value + step + 4, 4)

    def remote(src, dst, send, recv, target):
        return pltpu.make_async_remote_copy(
            src_ref=src, dst_ref=dst, send_sem=send, recv_sem=recv,
            device_id=target, device_id_type=MESH,
        )

    twin = device(x, y, z, 1 - c)

    def arrived(dst, recv):
        remote(dst, dst, l_s.at[0], recv, twin).wait_recv()

    def left(src, send):
        remote(src, src, send, l_r.at[0], twin).wait_send()

    def signal(target):
        pl.semaphore_signal(barrier, inc=1, device_id=target, device_id_type=MESH)

    barrier = pltpu.get_barrier_semaphore()
    for d in range(1, 16):
        other = lax.rem(x * 4 + y + d, 16)
        signal((other // 4, lax.rem(other, 4) * 8 + q))
    for d in range(1, 4):
        signal(device(x, turn(y, d), z, 1 - c))
        signal(device(x, turn(y, d), turn(z, -1), 1))
        signal(device(x, turn(y, d), turn(z, 1), 0))
    for d in range(1, 8):
        signal((x, y * 8 + lax.rem(q + d, 8)))
    masks = pack_masks(rsec, bond * 2)
    for w in range(TERMS):
        r_out[w] = packed_term(rband, w, masks)
    mine[...] = jnp.zeros_like(mine)
    pl.semaphore_wait(barrier, 31)

    above = as_int((z == 3) & (c == 1))
    below = as_int((z == 0) & (c == 0))
    halo_y = turn(y, above - below)
    halo_z = turn(z, 2 * c - 1)
    halo_slot = 3 * (1 - c)
    own_rows = pl.ds(pl.multiple_of(x * 32, 32), 32)

    def psi_columns(dy, k):
        return pl.ds(pl.multiple_of(dy * 1024 + k * 512, 512), 512)

    def psi_part(dy, k):
        return psi.at[own_rows, psi_columns(dy, k)]

    def psi_whole(dy, k):
        return psi.at[:, psi_columns(dy, k)]

    def psi_quarter(group, slot, part):
        return psi_in.at[group, slot, pl.ds(pl.multiple_of(part * 32, 32), 32)]

    for k in range(2):
        @pl.when(c == k)
        def _(k=k):
            pltpu.make_async_copy(
                psi_whole(y, k), psi_in.at[y, 1 + c], psi1_r.at[y * 4 + 1 + c]
            ).start()

        @pl.when(c != k)
        def _(k=k):
            remote(
                psi_whole(y, k), psi_in.at[y, 1 + c], psi1_s.at[k], psi1_r.at[y * 4 + 1 + c], twin
            ).start()

    for d in (1, 3, 2, 0):
        dy = turn(y, d)
        hy = turn(halo_y, d)
        for k in range(2):
            n = 2 * d + k
            if d > 0:
                remote(
                    psi_part(dy, k), psi_quarter(y, 1 + c, x), psi1_s.at[n],
                    psi1_r.at[y * 4 + 1 + c], device(x, dy, z, k),
                ).start()
                source, target = psi_part(hy, k), psi_quarter(halo_y, halo_slot, x)
            else:
                source, target = psi_whole(hy, k), psi_in.at[halo_y, halo_slot]
            remote(
                source, target, psi1_s.at[8 + n], psi1_r.at[halo_y * 4 + halo_slot],
                device(x, hy, halo_z, k),
            ).start()

    masks = pack_masks(lsec, bond * 2)
    number = lax.broadcasted_iota(jnp.int32, terms.shape, 1)
    active = []
    for h in range(2):
        same = 1 - jnp.clip(jnp.abs(number - lsec[bond * 2 + h]), 0, 1)
        active.append(jnp.sum(terms[...] * same, axis=1, keepdims=True))
    l_mine = l_in.at[y * 2 + c]
    for w in range(TERMS):
        switch = lanes_of(active[0][w : w + 1], active[1][w : w + 1]).astype(jnp.bfloat16)
        rows = (packed_term(lband, w, masks) * switch).T
        l_in[y * 2 + c, w] = jnp.concatenate([rows[:TILE], rows[TILE:]], axis=1)
    remote(l_mine, l_mine, l_s.at[0], l_r.at[1], device(x, turn(y, 1), z, c)).start()
    remote(l_mine, l_mine, l_s.at[1], l_r.at[3], device(x, turn(y, -1), z, c)).start()
    remote(l_mine, l_mine, lt_s.at[0], lt_r.at[0], twin).start()

    r_slot = lax.rem(z, 2) * 2 + c

    @pl.when(c == z // 2)
    def _():
        pltpu.make_async_copy(r_out, r_in.at[r_slot], r_r.at[r_slot]).start()

    @pl.when(c != z // 2)
    def _():
        remote(r_out, r_in.at[r_slot], r_s.at[0], r_r.at[r_slot], twin).start()

    for n, d in enumerate((1, -1)):
        remote(
            r_out, r_in.at[r_slot], r_s.at[1 + n], r_r.at[r_slot], device(x, y, turn(z, d), z // 2)
        ).start()

    order = [0, 1, 3, 2]

    def psi_strip(group, first, last, part):
        return psi_in.at[group, first:last, pl.ds(pl.multiple_of(part * 32, 32), 32)]

    def psi_second(k):
        group = turn(y, -order[k])
        for slot in range(4):
            arrived(psi_quarter(group, slot, x), psi1_r.at[group * 4 + slot])
        part = psi_strip(group, 0, 4, x)
        for n, d in enumerate((1, -1)):
            remote(
                part, part, psi2_s.at[2 * k + n], psi2_r.at[4 * n + group],
                device(turn(x, d), y, z, c),
            ).start()

    def psi_further(k):
        d = k + k // 2 - 2 * (k // 3)
        group = turn(y, -d)
        for n, d in enumerate((1, -1)):
            arrived(psi_strip(group, 0, 4, turn(x, -d)), psi2_r.at[4 * n + group])
            part = psi_strip(group, 2 * n, 2 * n + 2, turn(x, -d))
            remote(
                part, part, psi2_s.at[8 + 2 * k + n], psi2_r.at[8 + 4 * n + group],
                device(turn(x, d), y, z, c),
            ).start()

    def left_further():
        for n, d in enumerate((1, -1)):
            came = turn(y, -d) * 2 + c
            arrived(l_in.at[came], l_r.at[2 - d])
            remote(l_in.at[came], l_in.at[came], lt_s.at[2 - d], lt_r.at[2 - d], twin).start()
            part = l_in.at[came, :, 32 * n : 32 * n + 32]
            remote(
                part, part, l_s.at[2 + n], l_r.at[4 + n], device(x, turn(y, d), z, c)
            ).start()

    near = turn(z, (1 - 2 * lax.rem(z, 2)) * (1 - 2 * as_int(c != z // 2)))
    onward = turn(z, z - near)
    near_pair = lax.rem(near, 2) * 2
    half = as_int(onward != turn(z, 1))

    def right_part(first, which):
        return r_in.at[
            pl.ds(first, 2), :, pl.ds(pl.multiple_of(which * 96, 32), 96)
        ]

    def right_further():
        for n in range(2):
            arrived(r_in.at[near_pair + n], r_r.at[near_pair + n])
        part = right_part(near_pair, half)
        remote(part, part, r_s.at[3], rf_r.at[half], device(x, y, onward, c)).start()

    psi_second(1)
    psi_second(2)
    psi_second(3)
    psi_further(1)
    right_further()
    left_further()

    out[...] = jnp.zeros_like(out)
    gram_at = {}
    row = 5
    for k in range(4):
        for m in range(k, 4):
            gram_at[k, m] = row
            row += 1

    def gram(i, held):
        at = pl.ds(pl.multiple_of(i * 64, 64), 64)
        vectors = [sub[k, at, :].astype(jnp.float32) for k in range(4)]
        new = []
        for k in range(4):
            for m in range(k, 4):
                new.append(
                    held[len(new)]
                    + jnp.sum((vectors[k] * vectors[m]).reshape(8, 8, 128), axis=0)
                )
        return tuple(new)

    held = lax.fori_loop(
        0, 16, gram, tuple(jnp.zeros((8, 128), jnp.float32) for _ in range(10))
    )
    for k in range(10):
        mine[5 + k : 6 + k, :] = jnp.sum(held[k], axis=0, keepdims=True)

    def left_shard(group, core):
        for h in range(2):
            p = place_in_sector(lsec, group * 16 + z * 4 + core * 2 + h)
            weights = [
                (jnp.zeros((1, 256), jnp.int32) + as_int(p == at)).astype(jnp.bfloat16)
                for at in range(SEC_MOST)
            ]
            bands = l_in[group * 2 + core, :, :, h * PACKED : (h + 1) * PACKED].reshape(DEEP, PACKED)
            first = 2 + core * 2 + h
            rows = pl.ds(pl.multiple_of(group * 256 + core * 128 + h * TILE, TILE), TILE)
            for n in range(2):
                lanes = slice(n * 256, (n + 1) * 256)
                tiles = {
                    t: psi_in[group, t // 2, (t % 2) * TILE : (t % 2 + 1) * TILE, lanes]
                    for t in range(first - 2, first + 3)
                }
                source = jnp.concatenate(
                    [
                        tiles[first + m] * weights[0]
                        + tiles[first + m - 1] * weights[1]
                        + tiles[first + m - 2] * weights[2]
                        for m in range(SEC_MOST)
                    ],
                    axis=0,
                )
                made = jnp.dot(bands, source, preferred_element_type=jnp.float32).astype(
                    jnp.bfloat16
                )
                for w in range(TERMS):
                    mid[w, rows, lanes] = made[w * TILE : (w + 1) * TILE]

    def left_step(k, carry):
        d = k + k // 2 - 2 * (k // 3)
        group = turn(y, -d)
        own = l_in.at[group * 2 + c]

        @pl.when(k < 2)
        def _():
            psi_further(k + 2)

        @pl.when(k == 3)
        def _():
            for n in range(2):
                arrived(l_in.at[group * 2 + c, :, 32 * n : 32 * n + 32], l_r.at[4 + n])
            remote(own, own, lt_s.at[d], lt_r.at[d], twin).start()

        @pl.when(k == 0)
        def _():
            for slot in range(4):
                arrived(psi_in.at[y, slot], psi1_r.at[y * 4 + slot])

        @pl.when(k > 0)
        def _():
            for n in range(2):
                arrived(
                    psi_strip(group, 2 * n, 2 * n + 2, turn(x, 2)), psi2_r.at[8 + 4 * n + group]
                )

        arrived(l_in.at[group * 2 + 1 - c], lt_r.at[d])
        left_shard(group, 0)
        left_shard(group, 1)
        return carry

    lax.fori_loop(0, 4, left_step, 0)

    for d in range(4):
        zt = turn(z, d)
        part = sub.at[:, pl.ds(pl.multiple_of(zt * 256, 256), 256)]
        if d == 0:
            @pl.when(c == z // 2)
            def _(part=part):
                pltpu.make_async_copy(part, sub_in.at[r_slot], sub_r.at[r_slot]).start()

            @pl.when(c != z // 2)
            def _(part=part):
                remote(part, sub_in.at[r_slot], sub_s.at[0], sub_r.at[r_slot], twin).start()
        else:
            remote(
                part, sub_in.at[r_slot], sub_s.at[d], sub_r.at[r_slot], device(x, y, zt, z // 2)
            ).start()

    @pl.when(c == z // 2)
    def _():
        first = lax.rem(z, 2) * 2
        for n in range(2):
            arrived(r_in.at[first + n], r_r.at[first + n])

    @pl.when(c != z // 2)
    def _():
        for n in range(2):
            arrived(right_part(lax.rem(z, 2) * 2, n), rf_r.at[n])

    for b in range(4):
        place = [place_in_sector(rsec, y * 16 + c * 8 + b * 2 + h) for h in range(2)]
        weights = {}
        for i in range(6):
            for m in range(SEC_MOST):
                weights[i, m] = lanes_of(
                    as_int(place[0] == m - i + 2), as_int(place[1] == m - i + 3)
                ).astype(jnp.bfloat16)
        for w in range(TERMS):
            parts = [r_in[b, w, m * TILE : (m + 1) * TILE, :] for m in range(SEC_MOST)]
            for i in range(6):
                total = None
                for m in range(SEC_MOST):
                    if 0 <= m - i + 3 <= 3:
                        term = parts[m] * weights[i, m]
                        total = term if total is None else total + term
                r_wide[b, i * TILE : (i + 1) * TILE, w * 128 : (w + 1) * 128] = total

    def right_block(g, b):
        rows = pl.ds(pl.multiple_of(g * 256, 256), 256)
        source = jnp.concatenate(
            [mid[w, rows, b * 128 : (b + 1) * 128] for w in range(TERMS)], axis=1
        )
        out[rows, b * 128 : b * 128 + 384] += lax.dot_general(
            source, r_wide[b], (((1,), (1,)), ((), ())), preferred_element_type=jnp.float32
        )

    left_next = device(x, turn(y, -1 * as_int(c == 0)), z, 1 - c)
    right_next = device(x, turn(y, as_int(c == 1)), z, 1 - c)

    def right_step(i, carry):
        g = turn(x, i + 1)
        rows = pl.ds(pl.multiple_of(g * 256, 256), 256)
        right_block(g, 0)
        right_block(g, 3)
        right_block(g, 1)
        right_block(g, 2)

        @pl.when(i < 3)
        def _():
            rs_out[0, i] = out[rows, 256:512].astype(jnp.bfloat16)
            remote(
                rs_out.at[0, i], rs_in.at[0, i], rs_s.at[i], rs_r.at[i], device(g, y, z, c)
            ).start()

        halo_out[0, rows] = out[rows, 0:128].astype(jnp.bfloat16)
        halo_out[1, rows] = out[rows, 640:768].astype(jnp.bfloat16)
        remote(
            halo_out.at[0, rows], halo_in.at[1, rows], halo_s.at[i], halo_r.at[4 + i], left_next
        ).start()
        remote(
            halo_out.at[1, rows], halo_in.at[0, rows], halo_s.at[4 + i], halo_r.at[i], right_next
        ).start()

        return carry

    lax.fori_loop(0, 4, right_step, 0)

    def edge_columns(i, g):
        rows = pl.ds(pl.multiple_of(g * 256, 256), 256)
        for side in range(2):
            arrived(halo_in.at[side, rows], halo_r.at[4 * side + i])
        return (
            out[rows, 128:256] + halo_in[0, rows].astype(jnp.float32),
            out[rows, 512:640] + halo_in[1, rows].astype(jnp.float32),
        )

    def edge_step(i, carry):
        g = turn(x, i + 1)
        for n, total in enumerate(edge_columns(i, g)):
            rs_out[1, i, :, n * 128 : (n + 1) * 128] = total.astype(jnp.bfloat16)
        remote(
            rs_out.at[1, i], rs_in.at[1, i], rs_s.at[3 + i], rs_r.at[3 + i], device(g, y, z, c)
        ).start()
        return carry

    lax.fori_loop(0, 3, edge_step, 0)

    own_group = pl.ds(pl.multiple_of(x * 256, 256), 256)
    place_rows = pl.ds(pl.multiple_of(z * 256, 256), 256)
    held = [jnp.zeros((8, 128), jnp.float32) for _ in range(5)]
    for turn_of in range(2):
        if turn_of == 0:
            kept = (out[own_group, 256:384], out[own_group, 384:512])
        else:
            kept = edge_columns(3, x)
        for i in range(3):
            arrived(rs_in.at[turn_of, i], rs_r.at[3 * turn_of + i])
        for n in range(2):
            b = (1 + n) if turn_of == 0 else 3 * n
            total = kept[n]
            for i in range(3):
                total = total + rs_in[turn_of, i, :, n * 128 : (n + 1) * 128].astype(jnp.float32)
            zt, ct = 2 * c + b // 2, b % 2
            here = (z == zt) & (c == ct)

            @pl.when(here)
            def _(total=total):
                app[place_rows] = total

            @pl.when(jnp.logical_not(here))
            def _(total=total, b=b, zt=zt, ct=ct):
                deal[b] = total
                remote(
                    deal.at[b], app.at[place_rows], deal_s.at[b], deal_r.at[z],
                    device(x, y, zt, ct),
                ).start()

            arrived(sub_in.at[b], sub_r.at[b])
            products = [total * total] + [
                sub_in[b, k].astype(jnp.float32) * total for k in range(4)
            ]
            for k in range(5):
                held[k] = held[k] + jnp.sum(products[k].reshape(32, 8, 128), axis=0)
    for k in range(5):
        mine[k : k + 1, :] = jnp.sum(held[k], axis=0, keepdims=True)
    both = mine[...]
    both = both + pltpu.roll(both, TILE, 1)
    low_lanes = lax.broadcasted_iota(jnp.int32, (8, 128), 1) < TILE
    folded[...] = jnp.where(low_lanes, both[:8], both[8:])

    copies = []
    for d in range(1, 16):
        other = lax.rem(x * 4 + y + d, 16)
        copy = remote(
            folded, first_in.at[d - 1], send_c.at[d - 1], recv_c.at[d - 1],
            (other // 4, lax.rem(other, 4) * 8 + q),
        )
        copy.start()
        copies.append(copy)
    for copy in copies:
        copy.wait()
    added = folded[...]
    for d in range(15):
        added = added + first_in[d]
    second_out[...] = added
    copies = []
    for d in range(1, 8):
        copy = remote(
            second_out, second_in.at[d - 1], send_d.at[d - 1], recv_d.at[d - 1],
            (x, y * 8 + lax.rem(q + d, 8)),
        )
        copy.start()
        copies.append(copy)
    for copy in copies:
        copy.wait()
    for d in range(7):
        added = added + second_in[d]
    sums_all = jnp.concatenate(
        [
            jnp.sum(jnp.where(low_lanes, added, 0.0), axis=1, keepdims=True),
            jnp.sum(jnp.where(low_lanes, 0.0, added), axis=1, keepdims=True),
        ],
        axis=0,
    )

    def one(i):
        return sums_all[i : i + 1, :] * (1.0 / float(D_LEFT * D_RIGHT))

    coefficient = [one(1 + k) / (one(gram_at[k, k]) + epsilon) for k in range(4)]
    energy = one(0)
    for k in range(4):
        energy = energy - 2.0 * coefficient[k] * one(1 + k)
        for m in range(k, 4):
            twice = 1.0 if m == k else 2.0
            energy = energy + twice * coefficient[k] * coefficient[m] * one(gram_at[k, m])
    scale = lax.rsqrt(jnp.maximum(energy, 0.0) + epsilon)

    for i in range(4):
        @pl.when(jnp.logical_not((z == i) & (c == z // 2)))
        def _(i=i):
            arrived(app.at[i * 256 : (i + 1) * 256], deal_r.at[i])

    for n, value in enumerate(coefficient + [scale]):
        stats_ref[n : n + 1, :] = jnp.zeros((1, 128), jnp.float32) + value
    stats_ref[5:8, :] = jnp.zeros((3, 128), jnp.float32)

    for n in range(2):
        @pl.when(c != n)
        def _(n=n):
            left(psi_whole(y, n), psi1_s.at[n])

        left(psi_whole(y, n), psi1_s.at[8 + n])
    for n in range(2, 8):
        left(psi_part(y, 0), psi1_s.at[n])
        left(psi_part(y, 0), psi1_s.at[8 + n])

    @pl.when(c != z // 2)
    def _():
        left(r_out, r_s.at[0])
        left(sub.at[:, 0:256], sub_s.at[0])

    for d in range(1, 4):
        left(sub.at[:, 0:256], sub_s.at[d])
        left(rs_out.at[0, d - 1], rs_s.at[d - 1])
        left(rs_out.at[1, d - 1], rs_s.at[2 + d])
    for n in range(2, 8):
        left(psi_strip(0, 0, 4, x), psi2_s.at[n])
        left(psi_strip(0, 0, 2, x), psi2_s.at[8 + n])
    for n in range(2):
        left(l_mine, l_s.at[n])
        left(l_in.at[0, :, 0:32], l_s.at[2 + n])
        left(r_out, r_s.at[1 + n])
    left(right_part(near_pair, half), r_s.at[3])
    for g in range(4):
        left(l_mine, lt_s.at[g])
        left(halo_out.at[0, 0:256], halo_s.at[g])
        left(halo_out.at[1, 0:256], halo_s.at[4 + g])
        zt, ct = 2 * c + g // 2, g % 2

        @pl.when(jnp.logical_not((z == zt) & (c == ct)))
        def _(g=g):
            left(deal.at[g], deal_s.at[g])


def write_kernel(stats_ref, app_ref, sub_ref, applied_ref, vector_ref):
    residual = app_ref[...]
    applied_ref[...] = residual
    for k in range(4):
        residual = residual - stats_ref[k : k + 1, :] * sub_ref[k].astype(jnp.float32)
    vector_ref[...] = residual * stats_ref[4:5, :]


def per_device(
    wavefunction, subspace, left_band, right_band, left_sector, right_sector, term_sectors
):
    shape = jax.ShapeDtypeStruct((1024, 128), jnp.float32)
    dma = pltpu.SemaphoreType.DMA
    bf16, f32 = jnp.bfloat16, jnp.float32
    vmem = pl.BlockSpec(memory_space=pltpu.VMEM)
    smem = pl.BlockSpec(memory_space=pltpu.SMEM)
    app, stats = pl.pallas_call(
        kernel,
        out_shape=(shape, jax.ShapeDtypeStruct((8, 128), f32)),
        in_specs=[smem, smem, vmem, pl.BlockSpec(memory_space=pl.ANY), vmem, vmem, vmem],
        out_specs=(vmem, vmem),
        scratch_shapes=[
            pltpu.VMEM((8, TERMS, TILE, 2 * PACKED), bf16),
            pltpu.VMEM((TERMS, PACKED, 128), bf16),
            pltpu.VMEM((4, TERMS, PACKED, 128), bf16),
            pltpu.VMEM((4, 4, 128, 512), bf16),
            pltpu.VMEM((4, 384, TERMS * 128), bf16),
            pltpu.VMEM((TERMS, 1024, 512), bf16),
            pltpu.VMEM((1024, 768), f32),
            pltpu.VMEM((2, 1024, 128), bf16),
            pltpu.VMEM((2, 1024, 128), bf16),
            pltpu.VMEM((2, 3, 256, 256), bf16),
            pltpu.VMEM((2, 3, 256, 256), bf16),
            pltpu.VMEM((4, 4, 256, 128), bf16),
            pltpu.VMEM((4, 256, 128), f32),
            pltpu.VMEM((16, 128), f32),
            pltpu.VMEM((8, 128), f32),
            pltpu.VMEM((15, 8, 128), f32),
            pltpu.VMEM((8, 128), f32),
            pltpu.VMEM((7, 8, 128), f32),
            dma((16,)), dma((16,)), dma((16,)), dma((16,)),
            dma((4,)), dma((4,)), dma((2,)), dma((4,)), dma((6,)), dma((4,)), dma((4,)),
            dma((8,)), dma((8,)), dma((6,)), dma((6,)), dma((4,)), dma((4,)), dma((4,)), dma((4,)),
            dma((15,)), dma((15,)), dma((7,)), dma((7,)),
        ],
        compiler_params=pltpu.CompilerParams(
            collective_id=0, has_side_effects=True, vmem_limit_bytes=56 * 1024 * 1024
        ),
        name="two_site_step",
    )(
        left_sector, right_sector, term_sectors, wavefunction, subspace,
        jnp.swapaxes(left_band, 1, 2), jnp.swapaxes(right_band, 1, 2),
    )
    each = 512
    block = pl.BlockSpec((each, 128), lambda i: (i, 0))
    return pl.pallas_call(
        write_kernel,
        grid=(1024 // each,),
        out_shape=(shape, shape),
        in_specs=[
            pl.BlockSpec((8, 128), lambda i: (0, 0)),
            block,
            pl.BlockSpec((4, each, 128), lambda i: (0, i, 0)),
        ],
        out_specs=(block, block),
        name="write_results",
    )(stats, app, subspace)


def solution(mesh):
    return jax.shard_map(
        per_device,
        mesh=mesh,
        in_specs=(
            P("bond", None),
            P(None, "mpo", "bond"),
            P("mpo", "bond", None),
            P("mpo", "bond", None),
            P(),
            P(),
            P("mpo", None),
        ),
        out_specs=(P("mpo", "bond"), P("mpo", "bond")),
        check_vma=False,
    )
```
